128 devices in a mesh: src: 8 (over z_lo, y), tgt: 16 (over x, z_hi, core).
Axes of the slice: x: 4, y: 4, z: 4 (z_hi: 2, z_lo: 2; z = z_hi * 2 + z_lo), core: 2. Of those that a mesh axis runs over, the one named last changes fastest.
Arguments:
- charges: bfloat16 [2, 512, 1024, 512], P(None, ('src', 'tgt')), may hold values from -6 to 6
- source_xy: float32 [2, 512, 1024], P(None, ('src', 'tgt')), may hold values from 0 to 8
- target_xy: float32 [2, 128, 1024], P(None, ('src', 'tgt')), may hold values from 0 to 8
- anterp: bfloat16 [2, 512, 128, 1024], P(None, ('src', 'tgt')), may hold values from -0.1875 to 0.1875
- levels: bfloat16 [2, 2, 2, 512, 128, 128], P(None, None, None, ('src', 'tgt')), may hold values from -0.375 to 0.375
- transfer: bfloat16 [2, 128, 128, 8192], P(None, ('src', 'tgt')), may hold values from -0.0625 to 0.0625
- evaluate: bfloat16 [2, 128, 1024, 128], P(None, ('src', 'tgt')), may hold values from -0.5 to 0.5
- near_list: int32 [128, 3], P(('src', 'tgt')), may hold values from 0 to 3
Outputs:
- field: float32 [2, 128, 1024, 512], P(None, ('src', 'tgt'))
The draws below stay inside these ranges and needn't reach their ends.
Inputs may be any that keep to these rules, and one draw needn't show every extreme that they name: near_list[g, k] names one of the 4 source blocks of the device k - 1 columns further along tgt in g's quadtree row; entries naming a column outside the grid are ignored.
All inputs are finite; a program needn't handle non-finite values.
Results may differ from the reference program's by a relative error of at most 0.0065.
Values may be sent and summed in bfloat16 or wider, within the bound.
A program may use at most 256 MiB of HBM per device.

```python
import jax
import jax.numpy as jnp
from jax import lax

PTS = 1024
R = 128
NR = 512
SBLK = 4
TBLK = 1
LEVELS = 2
SB = 512
TB = 128
SCOLS = 8192
N_SRC = 8
N_TGT = 16


def with_ends(array, rng, low, largest):
    dims = array.shape
    index_at = [jax.random.randint(jax.random.fold_in(rng, axis), (), 0, dims[axis]) for axis in range(len(dims))]
    array = array.at[tuple(index_at)].set(low)
    longest = dims.index(max(dims))
    index_at[longest] = (index_at[longest] + 1) % dims[longest]
    return array.at[tuple(index_at)].set(largest)


def shard_levels(own_key, extent, pieces, least, high):
    def one(axis_at, parts):
        steps = jax.random.uniform(jax.random.fold_in(jax.random.fold_in(own_key, 6), axis_at), (parts,), jnp.float32, least / len(pieces), high / len(pieces))
        return jnp.repeat(jnp.exp(steps), extent[axis_at] // parts).reshape((-1,) + (1,) * (len(extent) - axis_at - 1))

    loudness = one(*pieces[0])
    for cut in pieces[1:]:
        loudness = loudness * one(*cut)
    return loudness


def normal_values(key, shape, spread, most, split=(), kind=jnp.bfloat16):
    drawn = jax.random.normal(key, shape, jnp.float32) * spread
    if len(split) > 0:
        drawn = shard_levels(key, shape, split, -0.22, 0.18) * drawn
    return jnp.clip(drawn, min=-most, max=most).astype(kind)


def setup_inputs(seed: int = 0) -> dict:
    key_of = jax.random.split(jax.random.key(seed), 9)
    charges = normal_values(key_of[0], (2, SB, PTS, NR), 1.0, 6.0, ((1, 128),))
    source_xy = jnp.clip(8.0 * jax.random.uniform(key_of[1], (2, SB, PTS), jnp.float32) ** shard_levels(key_of[1], (2, SB, PTS), ((1, 128),), -0.2, 0.2), 0.0, 8.0)
    target_xy = jnp.clip(8.0 * jax.random.uniform(key_of[2], (2, TB, PTS), jnp.float32) ** shard_levels(key_of[2], (2, TB, PTS), ((1, 128),), -0.2, 0.2), 0.0, 8.0)
    anterp = normal_values(key_of[3], (2, SB, R, PTS), PTS ** -0.5, 0.1875, ((1, 128),))
    levels = normal_values(key_of[4], (LEVELS, 2, 2, SB, R, R), (2 * R) ** -0.5, 0.375, ((3, 128),))
    transfer = normal_values(key_of[5], (2, TB, R, SCOLS), SCOLS ** -0.5, 0.0625, ((1, 128),))
    evaluate = normal_values(key_of[6], (2, TB, PTS, R), R ** -0.5, 0.5, ((1, 128),))
    near_list = with_ends(jax.random.randint(key_of[7], (TB, 3), 0, SBLK), jax.random.fold_in(key_of[7], 1), 0, SBLK - 1).astype(jnp.int32)
    return {"charges": charges, "source_xy": source_xy, "target_xy": target_xy, "anterp": anterp, "levels": levels, "transfer": transfer, "evaluate": evaluate, "near_list": near_list}


KAPPA = 73.27
CORE = 0.5
BOX = 8.0

def complex_apply(matrix, vector, form):
    left = matrix.astype(jnp.float32)
    right = vector.astype(jnp.float32)
    real_part = jnp.einsum(form, left[0], right[0]) - jnp.einsum(form, left[1], right[1])
    imag_part = jnp.einsum(form, left[0], right[1]) + jnp.einsum(form, left[1], right[0])
    return jnp.stack([real_part, imag_part])

def kernel_term(target_pos, source_pos, strengths):
    delta_x = target_pos[0][:, None] - source_pos[0][None, :]
    delta_y = target_pos[1][:, None] - source_pos[1][None, :]
    distance = jnp.sqrt(delta_x * delta_x + delta_y * delta_y + CORE * CORE)
    amplitude = 1.0 / (4.0 * jnp.pi * distance)
    phase = KAPPA * distance
    cosine = (amplitude * jnp.cos(phase)).astype(jnp.bfloat16)
    sine = (amplitude * jnp.sin(phase)).astype(jnp.bfloat16)
    real_part = jnp.dot(cosine, strengths[0], preferred_element_type=jnp.float32) - jnp.dot(sine, strengths[1], preferred_element_type=jnp.float32)
    imag_part = jnp.dot(cosine, strengths[1], preferred_element_type=jnp.float32) + jnp.dot(sine, strengths[0], preferred_element_type=jnp.float32)
    return jnp.stack([real_part, imag_part])

def reference(charges, source_xy, target_xy, anterp, levels, transfer, evaluate, near_list):
    blocks_row = N_TGT * SBLK
    mapped = lax.map(lambda pair: complex_apply(pair[0], pair[1], 'ij,jn->in'), (jnp.moveaxis(anterp, 1, 0), jnp.moveaxis(charges, 1, 0)))
    coeff = jnp.moveaxis(mapped, 0, 1).astype(jnp.bfloat16)
    row_ids = jnp.arange(N_SRC, dtype=jnp.int32)
    for level in range(LEVELS):
        stride = N_SRC >> level + 1
        grid = coeff.reshape(2, N_SRC, blocks_row, R, NR)
        partner = jnp.take(grid, row_ids ^ stride, axis=1).reshape(2, SB, R, NR)
        own_term = complex_apply(levels[level, 0], coeff, 'bij,bjn->bin')
        other_term = complex_apply(levels[level, 1], partner, 'bij,bjn->bin')
        coeff = (own_term + other_term).astype(jnp.bfloat16)
    grouped = coeff.reshape(2, N_SRC, SCOLS, NR)

    def one_target(target):
        row_src = target // (N_TGT * TBLK)
        col_tgt = target // TBLK % N_TGT
        weights = lax.dynamic_index_in_dim(transfer, target, 1, keepdims=False)
        column = lax.dynamic_index_in_dim(grouped, row_src, 1, keepdims=False)
        middle = complex_apply(weights, column, 'ij,jn->in').astype(jnp.bfloat16)
        result = complex_apply(lax.dynamic_index_in_dim(evaluate, target, 1, keepdims=False), middle, 'ij,jn->in')
        row_y = row_src.astype(jnp.float32) * BOX
        own_pos = lax.dynamic_index_in_dim(target_xy, target, 1, keepdims=False) + jnp.stack([col_tgt.astype(jnp.float32) * BOX, row_y])[:, None]
        for side in range(3):
            neighbour = col_tgt + side - 1
            inside = ((neighbour >= 0) & (neighbour < N_TGT)).astype(jnp.float32)
            clipped = jnp.clip(neighbour, 0, N_TGT - 1)
            block = ((row_src * N_TGT + clipped) * SBLK + near_list[target, side]).astype(jnp.int32)
            strengths = lax.dynamic_index_in_dim(charges, block, 1, keepdims=False)
            source_pos = lax.dynamic_index_in_dim(source_xy, block, 1, keepdims=False) + jnp.stack([neighbour.astype(jnp.float32) * BOX, row_y])[:, None]
            result = result + inside * kernel_term(own_pos, source_pos, strengths)
        return result
    fields = lax.map(one_target, jnp.arange(TB, dtype=jnp.int32))
    return jnp.moveaxis(fields, 0, 1)
```

```python
import functools
import math

import jax
import jax.numpy as jnp
from jax import lax
from jax.experimental import pallas as pl
from jax.experimental.pallas import tpu as pltpu
from jax.sharding import PartitionSpec as P

KAPPA = 73.27
CORE = 0.5
BOX = 8.0
MESH = pl.DeviceIdType.MESH
F32, BF16 = jnp.float32, jnp.bfloat16

PTS, R, NR, SBLK = 1024, 128, 512, 4
NC = 4
CW = NR // NC
ROWS = 128
PIECE = 256
NP = PTS // PIECE
COS = (0.99999922, -19.73898252, 64.92872657, -85.2723964, 58.79403555, -21.07677646)
SIN = (6.2830558, -41.33121426, 81.36681443, -74.47799927, 32.78139018)


def horner(coefs, u):
    out = coefs[-1]
    for c in coefs[-2::-1]:
        out = out * u + c
    return out


def cmul(top, bottom, x):
    d = jnp.dot(jnp.concatenate([top, bottom], 0), x, preferred_element_type=F32)
    m, n = top.shape[0], x.shape[1] // 2
    return d[:m, :n] - d[m:, n:], d[:m, n:] + d[m:, :n]


def lanes(k):
    if isinstance(k, int):
        return pl.ds(k * CW, CW)
    return pl.ds(pl.multiple_of(k * CW, CW), CW)


def rows_at(i, n):
    if isinstance(i, int):
        return pl.ds(i * n, n)
    return pl.ds(pl.multiple_of(i * n, n), n)


def gen_tile(txy, src, scale, row0, cos_ref, sin_ref, at):
    wide = 256

    def group(i, _):
        r = pl.ds(pl.multiple_of(row0 + i * 16, 16), 16)
        o = pl.ds(pl.multiple_of(at + i * 16, 16), 16)
        tx, ty = txy[r, 0:1], txy[r, 1:2]
        for j in range(PTS // wide):
            c = slice(j * wide, (j + 1) * wide)
            dx = tx - src[0:1, c]
            dy = ty - src[1:2, c]
            r2 = dx * dx + (dy * dy + CORE * CORE)
            inv = lax.rsqrt(r2)
            inv = inv * (1.5 - (0.5 * r2) * (inv * inv))
            turns = (r2 * inv) * (KAPPA / (2.0 * math.pi))
            f = turns - jnp.round(turns)
            u = f * f
            amp = inv * scale
            cos_ref[o, c] = (horner(COS, u) * amp).astype(BF16)
            sin_ref[o, c] = (horner(SIN, u) * (f * amp)).astype(BF16)
        return 0

    lax.fori_loop(0, ROWS // 16, group, 0)


def main_kernel(
    nlv, nls, sxy, txy, charges, anterp, levels, transfer, near_out, mid_out,
    ch, an, lv, w, v, g, ps, pr, ns, nr, sxs, sxr, sxo, nlr, nlm, tc, ts, toc, tos, acc,
    ld, lvs, nl_s, nl_r, nm_s, xs_s, xs_r, w_s, w_r, l_s, l_r, g_s, g_r, p_s, p_r, n_s, n_r, o_s,
):
    s, t = lax.axis_index("src"), lax.axis_index("tgt")
    n_src = 8
    c = t % 2
    hi = (t // 2) % 2
    x = t // 4
    sib = t + 1 - 2 * c
    far = (t + 15 + 2 * c) % 16
    def at(src, tgt):
        return {"src": src, "tgt": tgt}
    level_dev = [at((s + n_src // 2) % n_src, t), at(s // 4 * 4 + (s + 2) % 4, t)]
    z_dev = at(s, x * 4 + (1 - hi) * 2 + c)

    def x_dev(d, e):
        core = c if e == 0 else 1 - c
        return at(s, ((x + d) % 4) * 4 + hi * 2 + core)

    others = [(d, e) for d in (1, 3, 2, 0) for e in (0, 1) if (d, e) != (0, 0)]
    pending = []

    def remote(src, dst, ss, rs, dev):
        cp = pltpu.make_async_remote_copy(src, dst, ss, rs, device_id=dev, device_id_type=MESH)
        pending.append(cp)
        cp.start()
        return cp

    loads = []
    for b in range(SBLK):
        loads.append(pltpu.make_async_copy(charges.at[:, b], ch.at[:, b], ld.at[0, b]))
        loads.append(pltpu.make_async_copy(anterp.at[:, b], an.at[:, b], ld.at[1, b]))
    for cp in loads:
        cp.start()
    lv_loads = [
        pltpu.make_async_copy(levels.at[l, o], lv.at[l, :, :, :, pl.ds(o * R, R)], lvs.at[l, o])
        for l in range(2) for o in range(2)
    ]
    for cp in lv_loads:
        cp.start()

    greet = [x_dev(d, e) for d, e in others] + level_dev + [z_dev, at(s, far)]
    barrier = pltpu.get_barrier_semaphore()
    for dev in greet:
        pl.semaphore_signal(barrier, 1, device_id=dev, device_id_type=MESH)
    pl.semaphore_wait(barrier, len(greet))

    near_dev = [at(s, sib), at(s, far)]
    nl_cp = [remote(nlv.at[i], nlr.at[i], nl_s.at[i], nl_r.at[i], near_dev[i]) for i in range(2)]

    w_cp = {}
    own_w = []
    for h in range(2):
        col = (x * 4 + h * 2 + c) * (SBLK * R)
        own_w.append(pltpu.make_async_copy(
            transfer.at[:, 0, :, pl.ds(pl.multiple_of(col, SBLK * R), SBLK * R)],
            w.at[0, :, :, pl.ds(h * SBLK * R, SBLK * R)], w_s.at[0, h]))
        own_w[-1].start()

    def send_w(d, e):
        core = c if e == 0 else 1 - c
        slot = ((-d) % 4) * 2 + e
        for h in range(2):
            col = (((x + d) % 4) * 4 + h * 2 + core) * (SBLK * R)
            w_cp[slot, h] = remote(
                transfer.at[:, 0, :, pl.ds(pl.multiple_of(col, SBLK * R), SBLK * R)],
                w.at[slot, :, :, pl.ds(h * SBLK * R, SBLK * R)],
                w_s.at[slot, h], w_r.at[slot, h], x_dev(d, e))

    for d, e in others:
        send_w(d, e)

    for cp in loads:
        cp.wait()
    l_cp = {}

    def send_level(l, k):
        l_cp[l, k] = remote(
            v.at[l, k, :, pl.ds(0, R), :], v.at[l, k, :, pl.ds(R, R), :], l_s.at[l, k], l_r.at[l, k], level_dev[l])

    for k in range(NC):
        def block(b, _, k=k):
            xk = jnp.concatenate([ch[0, b, :, lanes(k)], ch[1, b, :, lanes(k)]], 1)
            re, im = cmul(an[0, b], an[1, b], xk)
            v[0, k, b, pl.ds(0, R), :] = jnp.concatenate([re, im], 1).astype(BF16)
            return 0
        lax.fori_loop(0, SBLK, block, 0)
        send_level(0, k)

    nm = []
    for i in range(2):
        nl_cp[i].wait_recv()
        nm.append(pltpu.make_async_copy(nlr.at[i], nlm.at[i], nm_s.at[i]))
        nm[i].start()
    xs_cp, n_cp = [], {}

    def pick(i):
        nm[i].wait()
        index = nlm[i, 0, 0]
        sxs[i] = sxy[index]

        def some(j, _):
            r = rows_at(j, 64)
            for q in range(2):
                ns[i, q, r, :] = ch[q, index, r, :]
            return 0

        lax.fori_loop(0, PTS // 64, some, 0)
        xs_cp.append(remote(sxs.at[i], sxr.at[i], xs_s.at[i], xs_r.at[i], near_dev[i]))

    def send_near(i, p):
        r = pl.ds(p * PIECE, PIECE)
        n_cp[i, p] = remote(ns.at[i, :, r, :], nr.at[i, :, r, :], n_s.at[i, p], n_r.at[i, p], near_dev[i])

    pick(1)
    send_near(1, 0)
    send_near(1, 1)
    pick(0)
    for p in range(NP):
        send_near(0, p)

    own = nls[0]
    amp = 1.0 / (4.0 * math.pi)
    sxo[...] = sxy[own]

    def own_rows(i):
        gen_tile(txy, sxo, amp, i * ROWS, toc, tos, 0)
        r = rows_at(i, ROWS)

        def chunk(k, _):
            xk = jnp.concatenate([ch[0, own, :, lanes(k)], ch[1, own, :, lanes(k)]], 1)
            re, im = cmul(toc[...], tos[...], xk)
            acc[0, r, lanes(k)] = re
            acc[1, r, lanes(k)] = im
            return 0

        lax.fori_loop(0, NC, chunk, 0)

    def level_step(l, k):
        l_cp[l, k].wait_recv()

        def block(b, _):
            re, im = cmul(lv[l, 0, b], lv[l, 1, b], v[l, k, b])
            out = jnp.concatenate([re, im], 1).astype(BF16)
            if l == 0:
                v[1, k, b, pl.ds(0, R), :] = out
            else:
                g[k, hi, rows_at(b, R), :] = out
            return 0

        lax.fori_loop(0, SBLK, block, 0)

    g_cp = {}
    for cp in lv_loads:
        cp.wait()
    for k in range(NC):
        own_rows(k)
        level_step(0, k)
        send_level(1, k)
    send_near(1, 2)
    for k in range(NC):
        own_rows(NC + k)
        level_step(1, k)
        g_cp[k] = remote(g.at[k, hi], g.at[k, hi], g_s.at[k], g_r.at[k], z_dev)
    send_near(1, 3)

    sib_off = BOX * (1 - 2 * c).astype(F32)
    far_amp = jnp.where((t == 0) | (t == 15), 0.0, amp)

    def side_tiles(i, first, count):
        def step(j, _):
            gen_tile(txy, sxr.at[i], amp if i == 0 else far_amp, (first + j) * ROWS, tc.at[i], ts.at[i], (first + j) * ROWS)
            return 0
        lax.fori_loop(0, count, step, 0)

    def side_part(i, p, out=False):
        cols = pl.ds(p * PIECE, PIECE)

        def row_step(j, _):
            r = rows_at(j, ROWS)

            def chunk(k, _):
                xk = jnp.concatenate([nr[i, 0, cols, lanes(k)], nr[i, 1, cols, lanes(k)]], 1)
                re, im = cmul(tc[i, r, cols], ts[i, r, cols], xk)
                acc[0, r, lanes(k)] += re
                acc[1, r, lanes(k)] += im
                return 0

            lax.fori_loop(0, NC, chunk, 0)
            return 0

        lax.fori_loop(0, PTS // ROWS, row_step, 0)

    for i in range(2):
        xs_cp[1 - i].wait_recv()
        sxr[i] = sxr[i] + jnp.where(lax.broadcasted_iota(jnp.int32, (2, PTS), 0) == 0, sib_off if i == 0 else -sib_off, 0.0)

    p_cp = {}

    def partial_step(k):
        g_cp[k].wait_recv()
        gk = g.at[k]

        def one(slot, _):
            xk = jnp.concatenate([gk[0], gk[1]], 0)
            re, im = cmul(w[slot, 0], w[slot, 1], xk)
            ps[k, slot] = jnp.concatenate([re, im], 1).astype(BF16)
            return 0

        lax.fori_loop(0, 8, one, 0)
        for d, e in others:
            slot = d * 2 + e
            back = ((-d) % 4) * 2 + e
            p_cp[k, back] = remote(ps.at[k, slot], pr.at[k, back], p_s.at[k, slot], p_r.at[k, back], x_dev(d, e))

    def middle_step(k):
        total = ps[k, 0].astype(F32)
        for d, e in others:
            back = d * 2 + e
            p_cp[k, back].wait_recv()
            total = total + pr[k, back].astype(F32)
        mid_out[k] = total.astype(BF16)

    side_tiles(0, 0, 8)
    for p in range(NP):
        n_cp[0, p].wait_recv()
        side_part(0, p)
    for cp in own_w:
        cp.wait()
    for cp in w_cp.values():
        cp.wait_recv()
    for k in range(NC):
        side_tiles(1, 2 * k, 2)
        partial_step(k)
    for k in range(NC):
        middle_step(k)
        n_cp[1, k].wait_recv()
        side_part(1, k)
    outs = pltpu.make_async_copy(acc, near_out, o_s)
    outs.start()
    outs.wait()
    for cp in pending:
        cp.wait_send()


def finish_kernel(near, evaluate, mid, out):
    er, ei = evaluate[0, 0], evaluate[1, 0]
    for k in range(NC):
        re, im = cmul(er, ei, mid[k])
        out[0, 0, :, k * CW:(k + 1) * CW] = near[0, :, k * CW:(k + 1) * CW] + re
        out[1, 0, :, k * CW:(k + 1) * CW] = near[1, :, k * CW:(k + 1) * CW] + im


def shards(charges, source_xy, target_xy, anterp, levels, transfer, evaluate, near_list):
    odd = lax.axis_index("tgt") % 2
    left, own, right = near_list[0, 0], near_list[0, 1], near_list[0, 2]
    to_sib = jnp.where(odd == 1, left, right)
    to_far = jnp.where(odd == 1, right, left)
    nlv = jnp.broadcast_to(jnp.stack([to_sib, to_far])[:, None, None], (2, 8, 128))
    nls = own[None]
    sxy = jnp.moveaxis(source_xy, 1, 0)
    txy = target_xy[:, 0, :].T
    vmem = pl.BlockSpec(memory_space=pltpu.VMEM)
    hbm = pl.BlockSpec(memory_space=pl.ANY)
    dma = pltpu.SemaphoreType.DMA
    near, mid = pl.pallas_call(
        main_kernel,
        out_shape=(
            jax.ShapeDtypeStruct((2, PTS, NR), F32),
            jax.ShapeDtypeStruct((NC, R, 2 * CW), BF16),
        ),
        in_specs=[vmem, pl.BlockSpec(memory_space=pltpu.SMEM), vmem, vmem, hbm, hbm, hbm, hbm],
        out_specs=(hbm, vmem),
        scratch_shapes=[
            pltpu.VMEM((2, SBLK, PTS, NR), BF16),
            pltpu.VMEM((2, SBLK, R, PTS), BF16),
            pltpu.VMEM((2, 2, SBLK, R, 2 * R), BF16),
            pltpu.VMEM((8, 2, R, 2 * SBLK * R), BF16),
            pltpu.VMEM((2, NC, SBLK, 2 * R, 2 * CW), BF16),
            pltpu.VMEM((NC, 2, SBLK * R, 2 * CW), BF16),
            pltpu.VMEM((NC, 8, R, 2 * CW), BF16),
            pltpu.VMEM((NC, 8, R, 2 * CW), BF16),
            pltpu.VMEM((2, 2, PTS, NR), BF16),
            pltpu.VMEM((2, 2, PTS, NR), BF16),
            pltpu.VMEM((2, 2, PTS), F32),
            pltpu.VMEM((2, 2, PTS), F32),
            pltpu.VMEM((2, PTS), F32),
            pltpu.VMEM((2, 8, 128), jnp.int32),
            pltpu.SMEM((2, 8, 128), jnp.int32),
            pltpu.VMEM((2, PTS, PTS), BF16),
            pltpu.VMEM((2, PTS, PTS), BF16),
            pltpu.VMEM((ROWS, PTS), BF16),
            pltpu.VMEM((ROWS, PTS), BF16),
            pltpu.VMEM((2, PTS, NR), F32),
            dma((2, SBLK)), dma((2, 2)), dma((2,)), dma((2,)), dma((2,)), dma((2,)), dma((2,)),
            dma((8, 2)), dma((8, 2)), dma((2, NC)), dma((2, NC)), dma((NC,)), dma((NC,)),
            dma((NC, 8)), dma((NC, 8)), dma((2, NP)), dma((2, NP)), dma,
        ],
        compiler_params=pltpu.CompilerParams(
            collective_id=0, has_side_effects=True, vmem_limit_bytes=60 * 2**20),
        name="exchange_and_near",
    )(nlv, nls, sxy, txy, charges, anterp, levels, transfer)
    rows = 256
    return pl.pallas_call(
        finish_kernel,
        grid=(PTS // rows,),
        out_shape=jax.ShapeDtypeStruct((2, 1, PTS, NR), F32),
        in_specs=[
            pl.BlockSpec((2, rows, NR), lambda i: (0, i, 0)),
            pl.BlockSpec((2, 1, rows, R), lambda i: (0, 0, i, 0)),
            pl.BlockSpec((NC, R, 2 * CW), lambda i: (0, 0, 0)),
        ],
        out_specs=pl.BlockSpec((2, 1, rows, NR), lambda i: (0, 0, i, 0)),
        name="evaluate_and_add",
    )(near, evaluate, mid)


def solution(mesh):
    return jax.shard_map(
        shards,
        mesh=mesh,
        in_specs=(
            P(None, ("src", "tgt"), None, None),
            P(None, ("src", "tgt"), None),
            P(None, ("src", "tgt"), None),
            P(None, ("src", "tgt"), None, None),
            P(None, None, None, ("src", "tgt"), None, None),
            P(None, ("src", "tgt"), None, None),
            P(None, ("src", "tgt"), None, None),
            P(("src", "tgt"), None),
        ),
        out_specs=P(None, ("src", "tgt"), None, None),
        check_vma=False,
    )
```

```python
import functools
import math

import jax
import jax.numpy as jnp
from jax import lax
from jax.experimental import pallas as pl
from jax.experimental.pallas import tpu as pltpu
from jax.sharding import PartitionSpec as P

KAPPA = 73.27
CORE = 0.5
BOX = 8.0
MESH = pl.DeviceIdType.MESH
F32, BF16 = jnp.float32, jnp.bfloat16

PTS, R, NR, SBLK = 1024, 128, 512, 4
KB = SBLK * R
NC = 2
CW = NR // NC
ROWS = 128
PIECE = 256
NP = PTS // PIECE
COS = (0.99999922, -19.73898252, 64.92872657, -85.2723964, 58.79403555, -21.07677646)
SIN = (6.2830558, -41.33121426, 81.36681443, -74.47799927, 32.78139018)


def horner(coefs, u):
    out = coefs[-1]
    for c in coefs[-2::-1]:
        out = out * u + c
    return out


def cdot(ar, ai, xr, xi):
    dot = functools.partial(jnp.dot, preferred_element_type=F32)
    return dot(ar, xr) - dot(ai, xi), dot(ar, xi) + dot(ai, xr)


def rows_at(i, n):
    if isinstance(i, int):
        return pl.ds(i * n, n)
    return pl.ds(pl.multiple_of(i * n, n), n)


def gen_tile(txy, src, scale, row0, cos_ref, sin_ref, at):
    wide = 256

    def group(i, _):
        r = pl.ds(pl.multiple_of(row0 + i * 16, 16), 16)
        o = pl.ds(pl.multiple_of(at + i * 16, 16), 16)
        tx, ty = txy[r, 0:1], txy[r, 1:2]
        for j in range(PTS // wide):
            c = slice(j * wide, (j + 1) * wide)
            dx = tx - src[0:1, c]
            dy = ty - src[1:2, c]
            r2 = dx * dx + (dy * dy + CORE * CORE)
            inv = lax.rsqrt(r2)
            inv = inv * (1.5 - (0.5 * r2) * (inv * inv))
            turns = (r2 * inv) * (KAPPA / (2.0 * math.pi))
            f = turns - jnp.round(turns)
            u = f * f
            amp = inv * scale
            cos_ref[o, c] = (horner(COS, u) * amp).astype(BF16)
            sin_ref[o, c] = (horner(SIN, u) * (f * amp)).astype(BF16)
        return 0

    lax.fori_loop(0, ROWS // 16, group, 0)


def main_kernel(
    near, sxy, txy, charges, anterp, levels, transfer, evaluate, out,
    ch, an, lv, w, v, g, ps, pr, mid, ev, ns, nr, nlv, nlr, nlm, sxs, sxr, txt, tc, ts, acc,
    ld, lvs, evs, nl_s, nl_r, nm_s, xs_s, xs_r, w_s, w_r, l_s, l_r, g_s, g_r, p_s, p_r, n_s, n_r, o_s,
):
    s, t = lax.axis_index("src"), lax.axis_index("tgt")
    n_src = 8
    c = t % 2
    hi = (t // 2) % 2
    x = t // 4

    def at(src, tgt):
        return {"src": src, "tgt": tgt}

    near_dev = [at(s, t + 1 - 2 * c), at(s, (t + 15 + 2 * c) % 16)]
    level_dev = [at((s + n_src // 2) % n_src, t), at(s // 4 * 4 + (s + 2) % 4, t)]
    z_dev = at(s, x * 4 + (1 - hi) * 2 + c)

    def x_dev(d, e):
        core = c if e == 0 else 1 - c
        return at(s, ((x + d) % 4) * 4 + hi * 2 + core)

    others = [(d, e) for d in (1, 3, 2, 0) for e in (0, 1) if (d, e) != (0, 0)]
    pending = []

    def remote(src, dst, ss, rs, dev):
        cp = pltpu.make_async_remote_copy(src, dst, ss, rs, device_id=dev, device_id_type=MESH)
        pending.append(cp)
        cp.start()
        return cp

    loads = []
    for b in range(SBLK):
        loads.append((
            pltpu.make_async_copy(anterp.at[:, b], an.at[:, b], ld.at[1, b]),
            pltpu.make_async_copy(charges.at[:, b], ch.at[:, b], ld.at[0, b])))
        for cp in loads[b]:
            cp.start()
    lv_loads = [
        pltpu.make_async_copy(levels.at[l, o], lv.at[l, :, :, :, pl.ds(o * R, R)], lvs.at[l, o])
        for l in range(2) for o in range(2)
    ]
    for cp in lv_loads:
        cp.start()
    ev_loads = [
        pltpu.make_async_copy(evaluate.at[q, 0], ev.at[:, pl.ds(q * R, R)], evs.at[q]) for q in range(2)
    ]
    for cp in ev_loads:
        cp.start()

    greet = [x_dev(d, e) for d, e in others] + level_dev + [z_dev, near_dev[1]]
    barrier = pltpu.get_barrier_semaphore()
    for dev in greet:
        pl.semaphore_signal(barrier, 1, device_id=dev, device_id_type=MESH)
    left, own, right = near[0, 0], near[0, 1], near[0, 2]
    nlv[0] = jnp.full((8, 128), jnp.where(c == 1, left, right), jnp.int32)
    nlv[1] = jnp.full((8, 128), jnp.where(c == 1, right, left), jnp.int32)
    pl.semaphore_wait(barrier, len(greet))
    nl_cp = [remote(nlv.at[i], nlr.at[i], nl_s.at[i], nl_r.at[i], near_dev[i]) for i in (1, 0)][::-1]

    w_cp = {}
    own_w = []
    for h in range(2):
        col = (x * 4 + h * 2 + c) * KB
        own_w.append(pltpu.make_async_copy(
            transfer.at[:, 0, :, pl.ds(pl.multiple_of(col, KB), KB)],
            w.at[:, pl.ds(0, R), pl.ds(h * KB, KB)], w_s.at[0, h]))

    def send_w(d, e):
        core = c if e == 0 else 1 - c
        slot = ((-d) % 4) * 2 + e
        for h in range(2):
            col = (((x + d) % 4) * 4 + h * 2 + core) * KB
            w_cp[slot, h] = remote(
                transfer.at[:, 0, :, pl.ds(pl.multiple_of(col, KB), KB)],
                w.at[:, pl.ds(slot * R, R), pl.ds(h * KB, KB)],
                w_s.at[slot, h], w_r.at[slot, h], x_dev(d, e))

    l_cp = {}

    def send_level(l, b):
        l_cp[l, b] = remote(
            v.at[l, b, :, pl.ds(0, R), :], v.at[l, b, :, pl.ds(R, R), :], l_s.at[l, b], l_r.at[l, b], level_dev[l])

    for b in range(SBLK):
        for cp in loads[b]:
            cp.wait()
        re, im = cdot(an[0, b], an[1, b], ch[0, b], ch[1, b])
        v[0, b, 0, pl.ds(0, R), :] = re.astype(BF16)
        v[0, b, 1, pl.ds(0, R), :] = im.astype(BF16)
        send_level(0, b)

    for d, e in others:
        send_w(d, e)
    for cp in own_w:
        cp.start()

    nm = {}
    for i in (1, 0):
        nl_cp[i].wait_recv()
        nm[i] = pltpu.make_async_copy(nlr.at[i], nlm.at[i], nm_s.at[i])
        nm[i].start()
    xs_cp, n_cp = {}, {}

    def pick(i):
        nm[i].wait()
        index = nlm[i, 0, 0]
        shift = BOX * (2 * c - 1).astype(F32)
        sxs[i, 0:1, :] = sxy[0, pl.ds(index, 1), :] + (shift if i == 0 else -shift)
        sxs[i, 1:2, :] = sxy[1, pl.ds(index, 1), :]

        def some(j, _):
            r = rows_at(j, 64)
            for q in range(2):
                ns[i, q, r, :] = ch[q, index, r, :]
            return 0

        lax.fori_loop(0, PTS // 64, some, 0)
        xs_cp[i] = remote(sxs.at[i], sxr.at[i], xs_s.at[i], xs_r.at[i], near_dev[i])

    def send_near(i, p):
        r = pl.ds(p * PIECE, PIECE)
        n_cp[i, p] = remote(ns.at[i, :, r, :], nr.at[i, :, r, :], n_s.at[i, p], n_r.at[i, p], near_dev[i])

    pick(1)
    for p in FAR_SENDS[0]:
        send_near(1, p)
    pick(0)
    for p in range(NP):
        send_near(0, p)

    amp = 1.0 / (4.0 * math.pi)
    txt[...] = jnp.concatenate([txy[0], txy[1], jnp.zeros((6, PTS), F32)], 0).T
    sxs[2, 0:1, :] = sxy[0, pl.ds(own, 1), :]
    sxs[2, 1:2, :] = sxy[1, pl.ds(own, 1), :]

    def tiles(i, src, scale, first, count):
        def step(j, _):
            at_row = (first + j) * ROWS
            gen_tile(txt, src, scale, at_row, tc.at[i], ts.at[i], at_row)
            return 0
        lax.fori_loop(0, count, step, 0)

    def own_part(first, count):
        def row_step(j, _):
            r = rows_at(first + j, 256)
            acc[0, r, :], acc[1, r, :] = cdot(tc[0, r, :], ts[0, r, :], ch[0, own], ch[1, own])
            return 0
        lax.fori_loop(0, count, row_step, 0)

    def level_step(l, b):
        l_cp[l, b].wait_recv()
        re, im = cdot(lv[l, 0, b], lv[l, 1, b], v[l, b, 0], v[l, b, 1])
        if l == 0:
            v[1, b, 0, pl.ds(0, R), :] = re.astype(BF16)
            v[1, b, 1, pl.ds(0, R), :] = im.astype(BF16)
        else:
            r = pl.ds(pl.multiple_of(hi * KB + b * R, R), R)
            g[0, r, :] = re.astype(BF16)
            g[1, r, :] = im.astype(BF16)

    g_cp = {}
    for cp in lv_loads:
        cp.wait()
    for b in range(SBLK):
        tiles(0, sxs.at[2], amp, 2 * b, 2)
        level_step(0, b)
        send_level(1, b)
        for p in FAR_SENDS[1 + b]:
            send_near(1, p)
    for b in range(SBLK):
        own_part(b, 1)
        level_step(1, b)
        r = pl.ds(pl.multiple_of(hi * KB + b * R, R), R)
        g_cp[b] = remote(g.at[:, r, :], g.at[:, r, :], g_s.at[b], g_r.at[b], z_dev)
        for p in FAR_SENDS[5 + b]:
            send_near(1, p)

    far_amp = jnp.where((t == 0) | (t == 15), 0.0, amp)

    def far_part(p, m=512, done=None):
        cols = pl.ds(p * PIECE, PIECE)

        def row_step(j, _):
            r = rows_at(j, m)
            re, im = cdot(tc[1, r, cols], ts[1, r, cols], nr[1, 0, cols, :], nr[1, 1, cols, :])
            acc[0, r, :] += re
            acc[1, r, :] += im
            if done is not None:
                done(r)
            return 0

        lax.fori_loop(0, PTS // m, row_step, 0)

    xs_cp[0].wait_recv()
    tiles(0, sxr.at[0], amp, 0, 8)
    for p in range(NP):
        n_cp[0, p].wait_recv()

    def sib_step(j, _):
        r = rows_at(j, 256)
        re, im = cdot(tc[0, r, :], ts[0, r, :], nr[0, 0], nr[0, 1])
        acc[0, r, :] += re
        acc[1, r, :] += im
        return 0

    lax.fori_loop(0, PTS // 256, sib_step, 0)
    xs_cp[1].wait_recv()
    tiles(1, sxr.at[1], far_amp, 0, 8)

    p_cp = {}
    for cp in own_w:
        cp.wait()
    for cp in w_cp.values():
        cp.wait_recv()
    for b in range(SBLK):
        g_cp[b].wait_recv()
    for k in range(NC):
        cols = pl.ds(k * CW, CW)
        for j in (1, 0):
            r = pl.ds(j * 4 * R, 4 * R)
            re, im = cdot(w[0, r, :], w[1, r, :], g[0, :, cols], g[1, :, cols])
            ps[k, pl.ds(4 * j, 4), 0] = re.astype(BF16).reshape(4, R, CW)
            ps[k, pl.ds(4 * j, 4), 1] = im.astype(BF16).reshape(4, R, CW)
            for d, e in others:
                if d // 2 == j:
                    back = ((-d) % 4) * 2 + e
                    slot = d * 2 + e
                    p_cp[k, back] = remote(
                        ps.at[k, slot], pr.at[k, back], p_s.at[k, slot], p_r.at[k, back], x_dev(d, e))

    def middle(k):
        cols = pl.ds(k * CW, CW)
        for d, e in others:
            p_cp[k, d * 2 + e].wait_recv()
        for q in range(2):
            total = ps[k, 0, q].astype(F32)
            for d, e in others:
                total = total + pr[k, d * 2 + e, q].astype(F32)
            if q == 0:
                mid[0, pl.ds(0, R), cols] = total.astype(BF16)
                mid[1, pl.ds(R, R), cols] = total.astype(BF16)
            else:
                mid[0, pl.ds(R, R), cols] = (-total).astype(BF16)
                mid[1, pl.ds(0, R), cols] = total.astype(BF16)

    def far_field():
        def row_step(j, _):
            r = rows_at(j, 512)
            for q in range(2):
                acc[q, r, :] += jnp.dot(ev[r, :], mid[q], preferred_element_type=F32)
            return 0
        lax.fori_loop(0, PTS // 512, row_step, 0)

    for p in range(NP - 1):
        n_cp[1, p].wait_recv()
        far_part(p)
    for cp in ev_loads:
        cp.wait()
    for k in range(NC):
        middle(k)
    far_field()
    n_cp[1, NP - 1].wait_recv()
    outs = []
    cols = pl.ds((NP - 1) * PIECE, PIECE)
    for j in range(4):
        r = pl.ds(j * 256, 256)
        re, im = cdot(tc[1, r, cols], ts[1, r, cols], nr[1, 0, cols, :], nr[1, 1, cols, :])
        acc[0, r, :] += re
        acc[1, r, :] += im
        outs.append(pltpu.make_async_copy(acc.at[:, r, :], out.at[:, 0, r, :], o_s.at[j]))
        outs[j].start()
    for cp in outs:
        cp.wait()
    for cp in pending:
        cp.wait_send()


FAR_SENDS = ((), (), (0,), (1,), (), (), (2,), (), (3,))


def shards(charges, source_xy, target_xy, anterp, levels, transfer, evaluate, near_list):
    vmem = pl.BlockSpec(memory_space=pltpu.VMEM)
    hbm = pl.BlockSpec(memory_space=pl.ANY)
    dma = pltpu.SemaphoreType.DMA
    return pl.pallas_call(
        main_kernel,
        out_shape=jax.ShapeDtypeStruct((2, 1, PTS, NR), F32),
        in_specs=[pl.BlockSpec(memory_space=pltpu.SMEM), vmem, vmem, hbm, hbm, hbm, hbm, hbm],
        out_specs=hbm,
        scratch_shapes=[
            pltpu.VMEM((2, SBLK, PTS, NR), BF16),
            pltpu.VMEM((2, SBLK, R, PTS), BF16),
            pltpu.VMEM((2, 2, SBLK, R, 2 * R), BF16),
            pltpu.VMEM((2, 8 * R, 2 * KB), BF16),
            pltpu.VMEM((2, SBLK, 2, 2 * R, NR), BF16),
            pltpu.VMEM((2, 2 * KB, NR), BF16),
            pltpu.VMEM((NC, 8, 2, R, CW), BF16),
            pltpu.VMEM((NC, 8, 2, R, CW), BF16),
            pltpu.VMEM((2, 2 * R, NR), BF16),
            pltpu.VMEM((PTS, 2 * R), BF16),
            pltpu.VMEM((2, 2, PTS, NR), BF16),
            pltpu.VMEM((2, 2, PTS, NR), BF16),
            pltpu.VMEM((2, 8, 128), jnp.int32),
            pltpu.VMEM((2, 8, 128), jnp.int32),
            pltpu.SMEM((2, 8, 128), jnp.int32),
            pltpu.VMEM((3, 2, PTS), F32),
            pltpu.VMEM((2, 2, PTS), F32),
            pltpu.VMEM((PTS, 8), F32),
            pltpu.VMEM((2, PTS, PTS), BF16),
            pltpu.VMEM((2, PTS, PTS), BF16),
            pltpu.VMEM((2, PTS, NR), F32),
            dma((2, SBLK)), dma((2, 2)), dma((2,)), dma((2,)), dma((2,)), dma((2,)), dma((2,)), dma((2,)),
            dma((8, 2)), dma((8, 2)), dma((2, SBLK)), dma((2, SBLK)), dma((SBLK,)), dma((SBLK,)),
            dma((NC, 8)), dma((NC, 8)), dma((2, NP)), dma((2, NP)), dma((4,)),
        ],
        compiler_params=pltpu.CompilerParams(
            collective_id=0, has_side_effects=True, vmem_limit_bytes=60 * 2**20),
        name="field_kernel",
    )(near_list, source_xy, target_xy, charges, anterp, levels, transfer, evaluate)


def solution(mesh):
    return jax.shard_map(
        shards,
        mesh=mesh,
        in_specs=(
            P(None, ("src", "tgt"), None, None),
            P(None, ("src", "tgt"), None),
            P(None, ("src", "tgt"), None),
            P(None, ("src", "tgt"), None, None),
            P(None, None, None, ("src", "tgt"), None, None),
            P(None, ("src", "tgt"), None, None),
            P(None, ("src", "tgt"), None, None),
            P(("src", "tgt"), None),
        ),
        out_specs=P(None, ("src", "tgt"), None, None),
        check_vma=False,
    )
```

```python
import functools
import math

import jax
import jax.numpy as jnp
from jax import lax
from jax.experimental import pallas as pl
from jax.experimental.pallas import tpu as pltpu
from jax.sharding import PartitionSpec as P

KAPPA = 73.27
CORE = 0.5
BOX = 8.0
MESH = pl.DeviceIdType.MESH
F32, BF16 = jnp.float32, jnp.bfloat16

PTS, R, NR, SBLK = 1024, 128, 512, 4
KB = SBLK * R
NC = 2
CW = NR // NC
ROWS = 128
PIECE = 256
NP = PTS // PIECE
COS = (0.99999922, -19.73898252, 64.92872657, -85.2723964, 58.79403555, -21.07677646)
SIN = (6.2830558, -41.33121426, 81.36681443, -74.47799927, 32.78139018)


def horner(coefs, u):
    out = coefs[-1]
    for c in coefs[-2::-1]:
        out = out * u + c
    return out


def cdot(ar, ai, xr, xi):
    dot = functools.partial(jnp.dot, preferred_element_type=F32)
    return dot(ar, xr) - dot(ai, xi), dot(ar, xi) + dot(ai, xr)


def rows_at(i, n):
    if isinstance(i, int):
        return pl.ds(i * n, n)
    return pl.ds(pl.multiple_of(i * n, n), n)


def gen_tile(txy, src, scale, row0, cos_ref, sin_ref, at):
    wide = 256

    def group(i, _):
        r = pl.ds(pl.multiple_of(row0 + i * 16, 16), 16)
        o = pl.ds(pl.multiple_of(at + i * 16, 16), 16)
        tx, ty = txy[r, 0:1], txy[r, 1:2]
        for j in range(PTS // wide):
            c = slice(j * wide, (j + 1) * wide)
            dx = tx - src[0:1, c]
            dy = ty - src[1:2, c]
            r2 = dx * dx + (dy * dy + CORE * CORE)
            inv = lax.rsqrt(r2)
            inv = inv * (1.5 - (0.5 * r2) * (inv * inv))
            turns = (r2 * inv) * (KAPPA / (2.0 * math.pi))
            f = turns - jnp.round(turns)
            u = f * f
            amp = inv * scale
            cos_ref[o, c] = (horner(COS, u) * amp).astype(BF16)
            sin_ref[o, c] = (horner(SIN, u) * (f * amp)).astype(BF16)
        return 0

    lax.fori_loop(0, ROWS // 16, group, 0)


def main_kernel(
    near, sxy, txy, charges, anterp, levels, transfer, evaluate, out,
    ch, an, lv, w, v, g, qs, qr, pf, ps, pr, mid, ev, ns, nr, nlv, nlr, nlm, sxs, sxr, txt, tc, ts, acc,
    ld, lvs, evs, nl_s, nl_r, nm_s, xs_s, xs_r, w_s, w_r, l_s, l_r, g_s, g_r, q_s, q_r, p_s, p_r, n_s, n_r, o_s,
):
    s, t = lax.axis_index("src"), lax.axis_index("tgt")
    n_src = 8
    c = t % 2
    hi = (t // 2) % 2
    x = t // 4

    def at(src, tgt):
        return {"src": src, "tgt": tgt}

    near_dev = [at(s, t + 1 - 2 * c), at(s, (t + 15 + 2 * c) % 16)]
    level_dev = [at((s + n_src // 2) % n_src, t), at(s // 4 * 4 + (s + 2) % 4, t)]
    z_dev = at(s, x * 4 + (1 - hi) * 2 + c)

    def x_dev(d, e):
        core = c if e == 0 else 1 - c
        return at(s, ((x + d) % 4) * 4 + hi * 2 + core)

    others = [(d, e) for d in (1, 3, 2, 0) for e in (0, 1) if (d, e) != (0, 0)]
    pending = []

    def remote(src, dst, ss, rs, dev):
        cp = pltpu.make_async_remote_copy(src, dst, ss, rs, device_id=dev, device_id_type=MESH)
        pending.append(cp)
        cp.start()
        return cp

    loads = []
    for b in range(SBLK):
        loads.append((
            pltpu.make_async_copy(anterp.at[:, b], an.at[:, b], ld.at[1, b]),
            pltpu.make_async_copy(charges.at[:, b], ch.at[:, b], ld.at[0, b])))
        for cp in loads[b]:
            cp.start()
    lv_loads = [
        pltpu.make_async_copy(levels.at[l, o], lv.at[l, :, :, :, pl.ds(o * R, R)], lvs.at[l, o])
        for l in range(2) for o in range(2)
    ]
    for cp in lv_loads:
        cp.start()
    ev_loads = [
        pltpu.make_async_copy(evaluate.at[q, 0], ev.at[:, pl.ds(q * R, R)], evs.at[q]) for q in range(2)
    ]
    for cp in ev_loads:
        cp.start()

    greet = [x_dev(d, e) for d, e in others] + level_dev + [z_dev, near_dev[1]]
    barrier = pltpu.get_barrier_semaphore()
    for dev in greet:
        pl.semaphore_signal(barrier, 1, device_id=dev, device_id_type=MESH)
    left, own, right = near[0, 0], near[0, 1], near[0, 2]
    nlv[0] = jnp.full((8, 128), jnp.where(c == 1, left, right), jnp.int32)
    nlv[1] = jnp.full((8, 128), jnp.where(c == 1, right, left), jnp.int32)
    pl.semaphore_wait(barrier, len(greet))
    nl_cp = [remote(nlv.at[i], nlr.at[i], nl_s.at[i], nl_r.at[i], near_dev[i]) for i in (1, 0)][::-1]

    w_cp = {}
    own_w = []
    for h in range(2):
        col = (x * 4 + h * 2 + c) * KB
        own_w.append(pltpu.make_async_copy(
            transfer.at[:, 0, :, pl.ds(pl.multiple_of(col, KB), KB)],
            w.at[:, pl.ds(0, R), pl.ds(h * KB, KB)], w_s.at[0, h]))

    def send_w(d, e):
        core = c if e == 0 else 1 - c
        slot = e * 4 + (-d) % 4
        for h in range(2):
            col = (((x + d) % 4) * 4 + h * 2 + core) * KB
            w_cp[slot, h] = remote(
                transfer.at[:, 0, :, pl.ds(pl.multiple_of(col, KB), KB)],
                w.at[:, pl.ds(slot * R, R), pl.ds(h * KB, KB)],
                w_s.at[slot, h], w_r.at[slot, h], x_dev(d, e))

    l_cp = {}

    def send_level(l, b):
        l_cp[l, b] = remote(
            v.at[l, b, :, pl.ds(0, R), :], v.at[l, b, :, pl.ds(R, R), :], l_s.at[l, b], l_r.at[l, b], level_dev[l])

    for b in range(SBLK):
        for cp in loads[b]:
            cp.wait()
        re, im = cdot(an[0, b], an[1, b], ch[0, b], ch[1, b])
        v[0, b, 0, pl.ds(0, R), :] = re.astype(BF16)
        v[0, b, 1, pl.ds(0, R), :] = im.astype(BF16)
        send_level(0, b)

    for d, e in others:
        send_w(d, e)
    for cp in own_w:
        cp.start()

    nm = {}
    for i in (1, 0):
        nl_cp[i].wait_recv()
        nm[i] = pltpu.make_async_copy(nlr.at[i], nlm.at[i], nm_s.at[i])
        nm[i].start()
    xs_cp, n_cp = {}, {}

    def pick(i):
        nm[i].wait()
        index = nlm[i, 0, 0]
        shift = BOX * (2 * c - 1).astype(F32)
        sxs[i, 0:1, :] = sxy[0, pl.ds(index, 1), :] + (shift if i == 0 else -shift)
        sxs[i, 1:2, :] = sxy[1, pl.ds(index, 1), :]

        def some(j, _):
            r = rows_at(j, 64)
            for q in range(2):
                ns[i, q, r, :] = ch[q, index, r, :]
            return 0

        lax.fori_loop(0, PTS // 64, some, 0)
        xs_cp[i] = remote(sxs.at[i], sxr.at[i], xs_s.at[i], xs_r.at[i], near_dev[i])

    def send_near(i, p):
        r = pl.ds(p * PIECE, PIECE)
        n_cp[i, p] = remote(ns.at[i, :, r, :], nr.at[i, :, r, :], n_s.at[i, p], n_r.at[i, p], near_dev[i])

    pick(1)
    for p in FAR_SENDS[0]:
        send_near(1, p)
    pick(0)
    for p in range(NP):
        send_near(0, p)

    amp = 1.0 / (4.0 * math.pi)
    txt[...] = jnp.concatenate([txy[0], txy[1], jnp.zeros((6, PTS), F32)], 0).T
    sxs[2, 0:1, :] = sxy[0, pl.ds(own, 1), :]
    sxs[2, 1:2, :] = sxy[1, pl.ds(own, 1), :]

    def tiles(i, src, scale, first, count):
        def step(j, _):
            at_row = (first + j) * ROWS
            gen_tile(txt, src, scale, at_row, tc.at[i], ts.at[i], at_row)
            return 0
        lax.fori_loop(0, count, step, 0)

    def own_part(first, count):
        def row_step(j, _):
            r = rows_at(first + j, 256)
            acc[0, r, :], acc[1, r, :] = cdot(tc[0, r, :], ts[0, r, :], ch[0, own], ch[1, own])
            return 0
        lax.fori_loop(0, count, row_step, 0)

    def level_step(l, b):
        l_cp[l, b].wait_recv()
        re, im = cdot(lv[l, 0, b], lv[l, 1, b], v[l, b, 0], v[l, b, 1])
        if l == 0:
            v[1, b, 0, pl.ds(0, R), :] = re.astype(BF16)
            v[1, b, 1, pl.ds(0, R), :] = im.astype(BF16)
        else:
            r = pl.ds(pl.multiple_of(hi * KB + b * R, R), R)
            g[0, r, :] = re.astype(BF16)
            g[1, r, :] = im.astype(BF16)

    g_cp = {}
    for cp in lv_loads:
        cp.wait()
    for b in range(SBLK):
        tiles(0, sxs.at[2], amp, 2 * b, 2)
        level_step(0, b)
        send_level(1, b)
        for p in FAR_SENDS[1 + b]:
            send_near(1, p)
    for b in range(SBLK):
        own_part(b, 1)
        level_step(1, b)
        r = pl.ds(pl.multiple_of(hi * KB + b * R, R), R)
        g_cp[b] = remote(g.at[:, r, :], g.at[:, r, :], g_s.at[b], g_r.at[b], z_dev)
        for p in FAR_SENDS[5 + b]:
            send_near(1, p)

    far_amp = jnp.where((t == 0) | (t == 15), 0.0, amp)

    def far_part(p, m=512, done=None):
        cols = pl.ds(p * PIECE, PIECE)

        def row_step(j, _):
            r = rows_at(j, m)
            re, im = cdot(tc[1, r, cols], ts[1, r, cols], nr[1, 0, cols, :], nr[1, 1, cols, :])
            acc[0, r, :] += re
            acc[1, r, :] += im
            if done is not None:
                done(r)
            return 0

        lax.fori_loop(0, PTS // m, row_step, 0)

    xs_cp[0].wait_recv()
    tiles(0, sxr.at[0], amp, 0, 8)
    for p in range(NP):
        n_cp[0, p].wait_recv()

    def sib_step(j, _):
        r = rows_at(j, 256)
        re, im = cdot(tc[0, r, :], ts[0, r, :], nr[0, 0], nr[0, 1])
        acc[0, r, :] += re
        acc[1, r, :] += im
        return 0

    lax.fori_loop(0, PTS // 256, sib_step, 0)
    xs_cp[1].wait_recv()
    tiles(1, sxr.at[1], far_amp, 0, 8)

    q_cp, p_cp = {}, {}
    for cp in own_w:
        cp.wait()
    for cp in w_cp.values():
        cp.wait_recv()
    for b in range(SBLK):
        g_cp[b].wait_recv()
    for p in FAR_SENDS[9]:
        send_near(1, p)

    def partial(e, k):
        cols = pl.ds(k * CW, CW)
        r = pl.ds(e * 4 * R, 4 * R)
        return cdot(w[0, r, :], w[1, r, :], g[0, :, cols], g[1, :, cols])

    def for_sibling(k):
        for q, part in enumerate(partial(1, k)):
            qs[k, :, q] = part.astype(BF16).reshape(4, R, CW)
        q_cp[k] = remote(qs.at[k], qr.at[k], q_s.at[k], q_r.at[k], near_dev[0])

    def for_targets(k):
        for q, part in enumerate(partial(0, k)):
            pf[q] = part.reshape(4, R, CW)
        q_cp[k].wait_recv()
        for q in range(2):
            ps[k, :, q] = (pf[q] + qr[k, :, q].astype(F32)).astype(BF16)
        for d in (1, 3, 2):
            p_cp[k, d] = remote(
                ps.at[k, d], pr.at[k, 4 - d], p_s.at[k, d], p_r.at[k, 4 - d], x_dev(d, 0))

    for k in range(NC):
        for_sibling(k)
    for k in range(NC):
        for_targets(k)

    def middle(k):
        cols = pl.ds(k * CW, CW)
        for d in (1, 2, 3):
            p_cp[k, d].wait_recv()
        for q in range(2):
            total = ps[k, 0, q].astype(F32)
            for d in (1, 2, 3):
                total = total + pr[k, d, q].astype(F32)
            if q == 0:
                mid[0, pl.ds(0, R), cols] = total.astype(BF16)
                mid[1, pl.ds(R, R), cols] = total.astype(BF16)
            else:
                mid[0, pl.ds(R, R), cols] = (-total).astype(BF16)
                mid[1, pl.ds(0, R), cols] = total.astype(BF16)

    def far_field():
        def row_step(j, _):
            r = rows_at(j, 512)
            for q in range(2):
                acc[q, r, :] += jnp.dot(ev[r, :], mid[q], preferred_element_type=F32)
            return 0
        lax.fori_loop(0, PTS // 512, row_step, 0)

    for p in range(NP - 1):
        n_cp[1, p].wait_recv()
        far_part(p)
    for cp in ev_loads:
        cp.wait()
    for k in range(NC):
        middle(k)
    far_field()
    n_cp[1, NP - 1].wait_recv()
    outs = []
    cols = pl.ds((NP - 1) * PIECE, PIECE)
    for j in range(4):
        r = pl.ds(j * 256, 256)
        re, im = cdot(tc[1, r, cols], ts[1, r, cols], nr[1, 0, cols, :], nr[1, 1, cols, :])
        acc[0, r, :] += re
        acc[1, r, :] += im
        outs.append(pltpu.make_async_copy(acc.at[:, r, :], out.at[:, 0, r, :], o_s.at[j]))
        outs[j].start()
    for cp in outs:
        cp.wait()
    for cp in pending:
        cp.wait_send()


FAR_SENDS = ((), (), (0,), (1,), (), (), (), (), (2,), (3,))


def shards(charges, source_xy, target_xy, anterp, levels, transfer, evaluate, near_list):
    vmem = pl.BlockSpec(memory_space=pltpu.VMEM)
    hbm = pl.BlockSpec(memory_space=pl.ANY)
    dma = pltpu.SemaphoreType.DMA
    return pl.pallas_call(
        main_kernel,
        out_shape=jax.ShapeDtypeStruct((2, 1, PTS, NR), F32),
        in_specs=[pl.BlockSpec(memory_space=pltpu.SMEM), vmem, vmem, hbm, hbm, hbm, hbm, hbm],
        out_specs=hbm,
        scratch_shapes=[
            pltpu.VMEM((2, SBLK, PTS, NR), BF16),
            pltpu.VMEM((2, SBLK, R, PTS), BF16),
            pltpu.VMEM((2, 2, SBLK, R, 2 * R), BF16),
            pltpu.VMEM((2, 8 * R, 2 * KB), BF16),
            pltpu.VMEM((2, SBLK, 2, 2 * R, NR), BF16),
            pltpu.VMEM((2, 2 * KB, NR), BF16),
            pltpu.VMEM((NC, 4, 2, R, CW), BF16),
            pltpu.VMEM((NC, 4, 2, R, CW), BF16),
            pltpu.VMEM((2, 4, R, CW), F32),
            pltpu.VMEM((NC, 4, 2, R, CW), BF16),
            pltpu.VMEM((NC, 4, 2, R, CW), BF16),
            pltpu.VMEM((2, 2 * R, NR), BF16),
            pltpu.VMEM((PTS, 2 * R), BF16),
            pltpu.VMEM((2, 2, PTS, NR), BF16),
            pltpu.VMEM((2, 2, PTS, NR), BF16),
            pltpu.VMEM((2, 8, 128), jnp.int32),
            pltpu.VMEM((2, 8, 128), jnp.int32),
            pltpu.SMEM((2, 8, 128), jnp.int32),
            pltpu.VMEM((3, 2, PTS), F32),
            pltpu.VMEM((2, 2, PTS), F32),
            pltpu.VMEM((PTS, 8), F32),
            pltpu.VMEM((2, PTS, PTS), BF16),
            pltpu.VMEM((2, PTS, PTS), BF16),
            pltpu.VMEM((2, PTS, NR), F32),
            dma((2, SBLK)), dma((2, 2)), dma((2,)), dma((2,)), dma((2,)), dma((2,)), dma((2,)), dma((2,)),
            dma((8, 2)), dma((8, 2)), dma((2, SBLK)), dma((2, SBLK)), dma((SBLK,)), dma((SBLK,)),
            dma((NC,)), dma((NC,)), dma((NC, 4)), dma((NC, 4)), dma((2, NP)), dma((2, NP)), dma((4,)),
        ],
        compiler_params=pltpu.CompilerParams(
            collective_id=0, has_side_effects=True, vmem_limit_bytes=60 * 2**20),
        name="field_kernel",
    )(near_list, source_xy, target_xy, charges, anterp, levels, transfer, evaluate)


def solution(mesh):
    return jax.shard_map(
        shards,
        mesh=mesh,
        in_specs=(
            P(None, ("src", "tgt"), None, None),
            P(None, ("src", "tgt"), None),
            P(None, ("src", "tgt"), None),
            P(None, ("src", "tgt"), None, None),
            P(None, None, None, ("src", "tgt"), None, None),
            P(None, ("src", "tgt"), None, None),
            P(None, ("src", "tgt"), None, None),
            P(("src", "tgt"), None),
        ),
        out_specs=P(None, ("src", "tgt"), None, None),
        check_vma=False,
    )
```

```python
import functools
import math

import jax
import jax.numpy as jnp
from jax import lax
from jax.experimental import pallas as pl
from jax.experimental.pallas import tpu as pltpu
from jax.sharding import PartitionSpec as P

KAPPA = 73.27
CORE = 0.5
BOX = 8.0
MESH = pl.DeviceIdType.MESH
F32, BF16 = jnp.float32, jnp.bfloat16

PTS, R, NR, SBLK = 1024, 128, 512, 4
KB = SBLK * R
NC = 2
CW = NR // NC
ROWS = 128
PIECE = 256
NP = PTS // PIECE
COS = (0.99999922, -19.73898252, 64.92872657, -85.2723964, 58.79403555, -21.07677646)
SIN = (6.2830558, -41.33121426, 81.36681443, -74.47799927, 32.78139018)


def horner(coefs, u):
    out = coefs[-1]
    for c in coefs[-2::-1]:
        out = out * u + c
    return out


def cdot(ar, ai, xr, xi):
    dot = functools.partial(jnp.dot, preferred_element_type=F32)
    return dot(ar, xr) - dot(ai, xi), dot(ar, xi) + dot(ai, xr)


def rows_at(i, n):
    if isinstance(i, int):
        return pl.ds(i * n, n)
    return pl.ds(pl.multiple_of(i * n, n), n)


def gen_tile(txy, src, scale, row0, cos_ref, sin_ref, at):
    wide = 256

    def group(i, _):
        r = pl.ds(pl.multiple_of(row0 + i * 16, 16), 16)
        o = pl.ds(pl.multiple_of(at + i * 16, 16), 16)
        tx, ty = txy[r, 0:1], txy[r, 1:2]
        for j in range(PTS // wide):
            c = slice(j * wide, (j + 1) * wide)
            dx = tx - src[0:1, c]
            dy = ty - src[1:2, c]
            r2 = dx * dx + (dy * dy + CORE * CORE)
            inv = lax.rsqrt(r2)
            inv = inv * (1.5 - (0.5 * r2) * (inv * inv))
            turns = (r2 * inv) * (KAPPA / (2.0 * math.pi))
            f = turns - jnp.round(turns)
            u = f * f
            amp = inv * scale
            cos_ref[o, c] = (horner(COS, u) * amp).astype(BF16)
            sin_ref[o, c] = (horner(SIN, u) * (f * amp)).astype(BF16)
        return 0

    lax.fori_loop(0, ROWS // 16, group, 0)


def main_kernel(
    near, sxy, txy, charges, anterp, levels, transfer, near_out, tile_out, piece_out, mid,
    ch, an, lv, w, v, g, qs, qr, pf, ps, pr, ns, nr, rl, nlv, nlr, nlm, sxs, sxr, txt, tc, ts, acc, rounded,
    ld, lvs, nl_s, nl_r, nm_s, xs_s, xs_r, w_s, w_r, l_s, l_r, g_s, g_r, q_s, q_r, p_s, p_r, n_s, n_r, rl_s, rl_r, o_s,
):
    s, t = lax.axis_index("src"), lax.axis_index("tgt")
    n_src = 8
    c = t % 2
    hi = (t // 2) % 2
    x = t // 4

    def at(src, tgt):
        return {"src": src, "tgt": tgt}

    near_dev = [at(s, t + 1 - 2 * c), at(s, (t + 15 + 2 * c) % 16)]
    level_dev = [at((s + n_src // 2) % n_src, t), at(s // 4 * 4 + (s + 2) % 4, t)]
    z_dev = at(s, x * 4 + (1 - hi) * 2 + c)

    has_far = (t != 0) & (t != 15)
    relay = jnp.logical_not(has_far)
    relayed = (t == 3) | (t == 12)
    crossing = hi == c
    direct = has_far & jnp.logical_not(relayed)
    relay_dev = at(s, jnp.where(x == 0, 3 - t, jnp.where(x == 3, 27 - t, t)))
    relay_target = at(s, jnp.where(x == 0, 4, 11))

    def x_dev(d, e):
        core = c if e == 0 else 1 - c
        return at(s, ((x + d) % 4) * 4 + hi * 2 + core)

    others = [(d, e) for d in (1, 3, 2, 0) for e in (0, 1) if (d, e) != (0, 0)]
    pending = []

    def remote(src, dst, ss, rs, dev, only=None):
        cp = pltpu.make_async_remote_copy(src, dst, ss, rs, device_id=dev, device_id_type=MESH)
        pending.append((only, cp))
        if only is None:
            cp.start()
        else:
            pl.when(only)(cp.start)
        return cp

    loads = []
    for b in range(SBLK):
        loads.append((
            pltpu.make_async_copy(anterp.at[:, b], an.at[:, b], ld.at[1, b]),
            pltpu.make_async_copy(charges.at[:, b], ch.at[:, b], ld.at[0, b])))
        if b < 2:
            for cp in loads[b]:
                cp.start()
    lv_loads = [
        pltpu.make_async_copy(levels.at[l, o], lv.at[l, :, :, :, pl.ds(o * R, R)], lvs.at[l, o])
        for l in range(2) for o in range(2)
    ]

    greet = [x_dev(d, e) for d, e in others] + level_dev + [z_dev, near_dev[1]]
    barrier = pltpu.get_barrier_semaphore()
    for dev in greet:
        pl.semaphore_signal(barrier, 1, device_id=dev, device_id_type=MESH)

    @pl.when(relay | relayed)
    def _():
        pl.semaphore_signal(barrier, 1, device_id=relay_dev, device_id_type=MESH)

    left, own, right = near[0, 0], near[0, 1], near[0, 2]
    nlv[0] = jnp.full((8, 128), jnp.where(c == 1, left, right), jnp.int32)
    nlv[1] = jnp.full((8, 128), jnp.where(c == 1, right, left), jnp.int32)

    def coefficients(b):
        for cp in loads[b]:
            cp.wait()
        for cp in loads[b + 2] if b + 2 < SBLK else lv_loads if b + 2 == SBLK else ():
            cp.start()
        re, im = cdot(an[0, b], an[1, b], ch[0, b], ch[1, b])
        v[0, b, 0, pl.ds(0, R), :] = re.astype(BF16)
        v[0, b, 1, pl.ds(0, R), :] = im.astype(BF16)

    coefficients(0)
    pl.semaphore_wait(barrier, len(greet) + (relay | relayed).astype(jnp.int32))
    nl_cp = [remote(nlv.at[i], nlr.at[i], nl_s.at[i], nl_r.at[i], near_dev[i]) for i in (1, 0)][::-1]

    w_cp = {}
    own_w = []
    for h in range(2):
        col = (x * 4 + h * 2 + c) * KB
        own_w.append(pltpu.make_async_copy(
            transfer.at[:, 0, :, pl.ds(pl.multiple_of(col, KB), KB)],
            w.at[:, pl.ds(0, R), pl.ds(h * KB, KB)], w_s.at[0, h]))

    def send_w(d, e):
        core = c if e == 0 else 1 - c
        slot = e * 4 + (-d) % 4
        for h in range(2):
            col = (((x + d) % 4) * 4 + h * 2 + core) * KB
            w_cp[slot, h] = remote(
                transfer.at[:, 0, :, pl.ds(pl.multiple_of(col, KB), KB)],
                w.at[:, pl.ds(slot * R, R), pl.ds(h * KB, KB)],
                w_s.at[slot, h], w_r.at[slot, h], x_dev(d, e))

    l_cp = {}

    def send_level(l, b):
        l_cp[l, b] = remote(
            v.at[l, b, :, pl.ds(0, R), :], v.at[l, b, :, pl.ds(R, R), :], l_s.at[l, b], l_r.at[l, b], level_dev[l])

    for b in range(SBLK):
        if b > 0:
            coefficients(b)
        send_level(0, b)

    for d, e in others:
        send_w(d, e)
    for cp in own_w:
        cp.start()

    nm = {}
    for i in (1, 0):
        nl_cp[i].wait_recv()
        nm[i] = pltpu.make_async_copy(nlr.at[i], nlm.at[i], nm_s.at[i])
        nm[i].start()
    xs_cp, n_cp, rl_cp = {}, {}, {}

    def pick(i):
        nm[i].wait()
        index = nlm[i, 0, 0]
        shift = BOX * (2 * c - 1).astype(F32)
        sxs[i, 0:1, :] = sxy[0, pl.ds(index, 1), :] + (shift if i == 0 else -shift)
        sxs[i, 1:2, :] = sxy[1, pl.ds(index, 1), :]

        def some(j, _):
            r = rows_at(j, 64)
            for q in range(2):
                ns[i, q, r, :] = ch[q, index, r, :]
            return 0

        lax.fori_loop(0, PTS // 64, some, 0)
        xs_cp[i] = remote(sxs.at[i], sxr.at[i], xs_s.at[i], xs_r.at[i], near_dev[i])

    def send_near(i, p, only=None):
        r = pl.ds(p * PIECE, PIECE)
        n_cp[i, p] = remote(
            ns.at[i, :, r, :], nr.at[i, :, r, :], n_s.at[i, p], n_r.at[i, p], near_dev[i], only)

    def send_crossing(p):
        if p < len(RELAYS):
            send_near(1, p, crossing & direct)
            r = pl.ds(p * PIECE, PIECE)
            rl_cp[p] = remote(ns.at[1, :, r, :], rl.at[p], n_s.at[1, p], rl_r.at[p], relay_dev, relayed)
        else:
            send_near(1, p, crossing & has_far)

    def pass_on(p):
        pl.when(relay)(rl_cp[p].wait_recv)
        r = pl.ds(p * PIECE, PIECE)
        remote(rl.at[p], nr.at[1, :, r, :], rl_s.at[p], n_r.at[1, p], relay_target, relay)

    def sends_at(place):
        for p in X_SENDS[place]:
            send_crossing(p)
        for p in Z_SENDS[place]:
            send_near(1, p, jnp.logical_not(crossing))
        for p, where in enumerate(RELAYS):
            if where == place:
                pass_on(p)

    pick(1)
    sends_at(0)
    pick(0)
    for p in range(NP):
        send_near(0, p)

    amp = 1.0 / (4.0 * math.pi)
    txt[...] = jnp.concatenate([txy[0], txy[1], jnp.zeros((6, PTS), F32)], 0).T
    sxs[2, 0:1, :] = sxy[0, pl.ds(own, 1), :]
    sxs[2, 1:2, :] = sxy[1, pl.ds(own, 1), :]

    def tiles(i, src, scale, first, count):
        def step(j, _):
            at_row = (first + j) * ROWS
            gen_tile(txt, src, scale, at_row, tc.at[i], ts.at[i], at_row)
            return 0
        lax.fori_loop(0, count, step, 0)

    def own_part(first, count):
        def row_step(j, _):
            r = rows_at(first + j, 256)
            acc[0, r, :], acc[1, r, :] = cdot(tc[0, r, :], ts[0, r, :], ch[0, own], ch[1, own])
            return 0
        lax.fori_loop(0, count, row_step, 0)

    def level_step(l, b):
        l_cp[l, b].wait_recv()
        re, im = cdot(lv[l, 0, b], lv[l, 1, b], v[l, b, 0], v[l, b, 1])
        if l == 0:
            v[1, b, 0, pl.ds(0, R), :] = re.astype(BF16)
            v[1, b, 1, pl.ds(0, R), :] = im.astype(BF16)
        else:
            r = pl.ds(pl.multiple_of(hi * KB + b * R, R), R)
            g[0, r, :] = re.astype(BF16)
            g[1, r, :] = im.astype(BF16)

    g_cp = {}
    for cp in lv_loads:
        cp.wait()
    for b in range(SBLK):
        tiles(0, sxs.at[2], amp, 2 * b, 2)
        level_step(0, b)
        send_level(1, b)
        sends_at(1 + b)
    for b in range(SBLK):
        own_part(b, 1)
        level_step(1, b)
        r = pl.ds(pl.multiple_of(hi * KB + b * R, R), R)
        g_cp[b] = remote(g.at[:, r, :], g.at[:, r, :], g_s.at[b], g_r.at[b], z_dev)
        sends_at(5 + b)

    far_amp = jnp.where((t == 0) | (t == 15), 0.0, amp)

    def far_part(p):
        cols = pl.ds(p * PIECE, PIECE)

        def row_step(j, _):
            r = rows_at(j, 512)
            re, im = cdot(tc[1, r, cols], ts[1, r, cols], nr[1, 0, cols, :], nr[1, 1, cols, :])
            acc[0, r, :] += re
            acc[1, r, :] += im
            return 0

        n_cp[1, p].wait_recv()
        lax.fori_loop(0, PTS // 512, row_step, 0)

    xs_cp[0].wait_recv()
    tiles(0, sxr.at[0], amp, 0, 8)
    for p in range(NP):
        n_cp[0, p].wait_recv()

    def sib_step(j, _):
        r = rows_at(j, 256)
        re, im = cdot(tc[0, r, :], ts[0, r, :], nr[0, 0], nr[0, 1])
        acc[0, r, :] += re
        acc[1, r, :] += im
        return 0

    lax.fori_loop(0, PTS // 256, sib_step, 0)
    xs_cp[1].wait_recv()
    tiles(1, sxr.at[1], far_amp, 0, 8)
    last = pl.ds((NP - 1) * PIECE, PIECE)
    outs = [
        pltpu.make_async_copy(tc.at[1, :, last], tile_out.at[0], o_s.at[0]),
        pltpu.make_async_copy(ts.at[1, :, last], tile_out.at[1], o_s.at[1]),
    ]
    for cp in outs:
        cp.start()

    q_cp, p_cp = {}, {}
    for cp in own_w:
        cp.wait()
    for cp in w_cp.values():
        cp.wait_recv()
    for b in range(SBLK):
        g_cp[b].wait_recv()
    sends_at(9)

    def partial(e, k):
        cols = pl.ds(k * CW, CW)
        r = pl.ds(e * 4 * R, 4 * R)
        return cdot(w[0, r, :], w[1, r, :], g[0, :, cols], g[1, :, cols])

    def for_sibling(k):
        for q, part in enumerate(partial(1, k)):
            qs[k, :, q] = part.astype(BF16).reshape(4, R, CW)
        q_cp[k] = remote(qs.at[k], qr.at[k], q_s.at[k], q_r.at[k], near_dev[0])

    def for_targets(k):
        for q, part in enumerate(partial(0, k)):
            pf[q] = part.reshape(4, R, CW)
        q_cp[k].wait_recv()
        for q in range(2):
            ps[k, :, q] = (pf[q] + qr[k, :, q].astype(F32)).astype(BF16)
        for d in (1, 3, 2):
            p_cp[k, d] = remote(
                ps.at[k, d], pr.at[k, 4 - d], p_s.at[k, d], p_r.at[k, 4 - d], x_dev(d, 0))

    for k in range(NC):
        for_sibling(k)
    for k in range(NC):
        for_targets(k)

    def middle(k):
        cols = pl.ds(k * CW, CW)
        for d in (1, 2, 3):
            p_cp[k, d].wait_recv()
        for q in range(2):
            total = ps[k, 0, q].astype(F32)
            for d in (1, 2, 3):
                total = total + pr[k, d, q].astype(F32)
            if q == 0:
                mid[0, pl.ds(0, R), cols] = total.astype(BF16)
                mid[1, pl.ds(R, R), cols] = total.astype(BF16)
            else:
                mid[0, pl.ds(R, R), cols] = (-total).astype(BF16)
                mid[1, pl.ds(0, R), cols] = total.astype(BF16)

    for p in range(NP - 1):
        pl.when(has_far)(functools.partial(far_part, p))
    rounded[...] = acc[...].astype(BF16)
    outs.append(pltpu.make_async_copy(rounded, near_out, o_s.at[2]))
    outs[2].start()
    for k in range(NC):
        middle(k)

    @pl.when(relay)
    def _():
        nr[1, :, last, :] = jnp.zeros((2, PIECE, NR), BF16)

    pl.when(has_far)(n_cp[1, NP - 1].wait_recv)
    outs.append(pltpu.make_async_copy(nr.at[1, :, last, :], piece_out, o_s.at[3]))
    outs[3].start()
    for cp in outs:
        cp.wait()
    for only, cp in pending:
        if only is None:
            cp.wait_send()
        else:
            pl.when(only)(cp.wait_send)


def finish_kernel(near, tile, piece, mid, evaluate, out):
    dot = functools.partial(jnp.dot, preferred_element_type=F32)
    re, im = cdot(tile[0], tile[1], piece[0], piece[1])
    ev = jnp.concatenate([evaluate[0, 0], evaluate[1, 0]], 1)
    out[0, 0] = near[0].astype(F32) + re + dot(ev, mid[0])
    out[1, 0] = near[1].astype(F32) + im + dot(ev, mid[1])


RELAYS = (7, 8)
X_SENDS = ((), (0,), (1,), (2,), (), (3,), (), (), (), ())
Z_SENDS = ((), (), (), (), (), (), (), (), (0,), (1, 2, 3))


def shards(charges, source_xy, target_xy, anterp, levels, transfer, evaluate, near_list):
    vmem = pl.BlockSpec(memory_space=pltpu.VMEM)
    hbm = pl.BlockSpec(memory_space=pl.ANY)
    dma = pltpu.SemaphoreType.DMA
    near, tile, piece, mid = pl.pallas_call(
        main_kernel,
        out_shape=(
            jax.ShapeDtypeStruct((2, PTS, NR), BF16),
            jax.ShapeDtypeStruct((2, PTS, PIECE), BF16),
            jax.ShapeDtypeStruct((2, PIECE, NR), BF16),
            jax.ShapeDtypeStruct((2, 2 * R, NR), BF16),
        ),
        in_specs=[pl.BlockSpec(memory_space=pltpu.SMEM), vmem, vmem, hbm, hbm, hbm, hbm],
        out_specs=(hbm, hbm, hbm, vmem),
        scratch_shapes=[
            pltpu.VMEM((2, SBLK, PTS, NR), BF16),
            pltpu.VMEM((2, SBLK, R, PTS), BF16),
            pltpu.VMEM((2, 2, SBLK, R, 2 * R), BF16),
            pltpu.VMEM((2, 8 * R, 2 * KB), BF16),
            pltpu.VMEM((2, SBLK, 2, 2 * R, NR), BF16),
            pltpu.VMEM((2, 2 * KB, NR), BF16),
            pltpu.VMEM((NC, 4, 2, R, CW), BF16),
            pltpu.VMEM((NC, 4, 2, R, CW), BF16),
            pltpu.VMEM((2, 4, R, CW), F32),
            pltpu.VMEM((NC, 4, 2, R, CW), BF16),
            pltpu.VMEM((NC, 4, 2, R, CW), BF16),
            pltpu.VMEM((2, 2, PTS, NR), BF16),
            pltpu.VMEM((2, 2, PTS, NR), BF16),
            pltpu.VMEM((2, 2, PIECE, NR), BF16),
            pltpu.VMEM((2, 8, 128), jnp.int32),
            pltpu.VMEM((2, 8, 128), jnp.int32),
            pltpu.SMEM((2, 8, 128), jnp.int32),
            pltpu.VMEM((3, 2, PTS), F32),
            pltpu.VMEM((2, 2, PTS), F32),
            pltpu.VMEM((PTS, 8), F32),
            pltpu.VMEM((2, PTS, PTS), BF16),
            pltpu.VMEM((2, PTS, PTS), BF16),
            pltpu.VMEM((2, PTS, NR), F32),
            pltpu.VMEM((2, PTS, NR), BF16),
            dma((2, SBLK)), dma((2, 2)), dma((2,)), dma((2,)), dma((2,)), dma((2,)), dma((2,)),
            dma((8, 2)), dma((8, 2)), dma((2, SBLK)), dma((2, SBLK)), dma((SBLK,)), dma((SBLK,)),
            dma((NC,)), dma((NC,)), dma((NC, 4)), dma((NC, 4)), dma((2, NP)), dma((2, NP)), dma((2,)), dma((2,)), dma((4,)),
        ],
        compiler_params=pltpu.CompilerParams(
            collective_id=0, has_side_effects=True, vmem_limit_bytes=60 * 2**20),
        name="field_kernel",
    )(near_list, source_xy, target_xy, charges, anterp, levels, transfer)
    rows = 256
    return pl.pallas_call(
        finish_kernel,
        grid=(PTS // rows,),
        out_shape=jax.ShapeDtypeStruct((2, 1, PTS, NR), F32),
        in_specs=[
            pl.BlockSpec((2, rows, NR), lambda i: (0, i, 0)),
            pl.BlockSpec((2, rows, PIECE), lambda i: (0, i, 0)),
            pl.BlockSpec((2, PIECE, NR), lambda i: (0, 0, 0)),
            pl.BlockSpec((2, 2 * R, NR), lambda i: (0, 0, 0)),
            pl.BlockSpec((2, 1, rows, R), lambda i: (0, 0, i, 0)),
        ],
        out_specs=pl.BlockSpec((2, 1, rows, NR), lambda i: (0, 0, i, 0)),
        compiler_params=pltpu.CompilerParams(vmem_limit_bytes=60 * 2**20),
        name="finish_kernel",
    )(near, tile, piece, mid, evaluate)


def solution(mesh):
    return jax.shard_map(
        shards,
        mesh=mesh,
        in_specs=(
            P(None, ("src", "tgt"), None, None),
            P(None, ("src", "tgt"), None),
            P(None, ("src", "tgt"), None),
            P(None, ("src", "tgt"), None, None),
            P(None, None, None, ("src", "tgt"), None, None),
            P(None, ("src", "tgt"), None, None),
            P(None, ("src", "tgt"), None, None),
            P(("src", "tgt"), None),
        ),
        out_specs=P(None, ("src", "tgt"), None, None),
        check_vma=False,
    )
```

```python
import functools
import math

import jax
import jax.numpy as jnp
from jax import lax
from jax.experimental import pallas as pl
from jax.experimental.pallas import tpu as pltpu
from jax.sharding import PartitionSpec as P

KAPPA = 73.27
CORE = 0.5
BOX = 8.0
MESH = pl.DeviceIdType.MESH
F32, BF16 = jnp.float32, jnp.bfloat16

PTS, R, NR, SBLK = 1024, 128, 512, 4
KB = SBLK * R
NC = 2
CW = NR // NC
ROWS = 128
PIECE = 256
NP = PTS // PIECE
COS = (0.99999922, -19.73898252, 64.92872657, -85.2723964, 58.79403555, -21.07677646)
SIN = (6.2830558, -41.33121426, 81.36681443, -74.47799927, 32.78139018)


def horner(coefs, u):
    out = coefs[-1]
    for c in coefs[-2::-1]:
        out = out * u + c
    return out


def cdot(ar, ai, xr, xi):
    dot = functools.partial(jnp.dot, preferred_element_type=F32)
    return dot(ar, xr) - dot(ai, xi), dot(ar, xi) + dot(ai, xr)


def rows_at(i, n):
    if isinstance(i, int):
        return pl.ds(i * n, n)
    return pl.ds(pl.multiple_of(i * n, n), n)


def gen_tile(txy, src, scale, row0, cos_ref, sin_ref, at):
    wide = 256

    def group(i, _):
        r = pl.ds(pl.multiple_of(row0 + i * 16, 16), 16)
        o = pl.ds(pl.multiple_of(at + i * 16, 16), 16)
        tx, ty = txy[r, 0:1], txy[r, 1:2]
        for j in range(PTS // wide):
            c = slice(j * wide, (j + 1) * wide)
            dx = tx - src[0:1, c]
            dy = ty - src[1:2, c]
            r2 = dx * dx + (dy * dy + CORE * CORE)
            inv = lax.rsqrt(r2)
            inv = inv * (1.5 - (0.5 * r2) * (inv * inv))
            turns = (r2 * inv) * (KAPPA / (2.0 * math.pi))
            f = turns - jnp.round(turns)
            u = f * f
            amp = inv * scale
            cos_ref[o, c] = (horner(COS, u) * amp).astype(BF16)
            sin_ref[o, c] = (horner(SIN, u) * (f * amp)).astype(BF16)
        return 0

    lax.fori_loop(0, ROWS // 16, group, 0)


def main_kernel(
    near, sxy, txy, charges, anterp, levels, transfer, near_out, tile_out, piece_out, mid,
    ch, an, lv, w, v, g, qs, qr, pf, ps, pr, ns, nr, rl, nlv, nlr, nlm, sxs, sxr, txt, tc, ts, acc, rounded,
    ld, lvs, nl_s, nl_r, nm_s, xs_s, xs_r, w_s, w_r, l_s, l_r, g_s, g_r, q_s, q_r, p_s, p_r, n_s, n_r, rl_s, rl_r, o_s,
):
    s, t = lax.axis_index("src"), lax.axis_index("tgt")
    n_src = 8
    c = t % 2
    hi = (t // 2) % 2
    x = t // 4

    def at(src, tgt):
        return {"src": src, "tgt": tgt}

    near_dev = [at(s, t + 1 - 2 * c), at(s, (t + 15 + 2 * c) % 16)]
    level_dev = [at((s + n_src // 2) % n_src, t), at(s // 4 * 4 + (s + 2) % 4, t)]
    z_dev = at(s, x * 4 + (1 - hi) * 2 + c)

    has_far = (t != 0) & (t != 15)
    relay = jnp.logical_not(has_far)
    relayed = (t == 3) | (t == 12)
    crossing = hi == c
    direct = has_far & jnp.logical_not(relayed)
    relay_dev = at(s, jnp.where(x == 0, 3 - t, jnp.where(x == 3, 27 - t, t)))
    relay_target = at(s, jnp.where(x == 0, 4, 11))

    def x_dev(d, e):
        core = c if e == 0 else 1 - c
        return at(s, ((x + d) % 4) * 4 + hi * 2 + core)

    others = [(d, e) for d in (1, 3, 2, 0) for e in (0, 1) if (d, e) != (0, 0)]
    pending = []

    def remote(src, dst, ss, rs, dev, only=None):
        cp = pltpu.make_async_remote_copy(src, dst, ss, rs, device_id=dev, device_id_type=MESH)
        pending.append((only, cp))
        if only is None:
            cp.start()
        else:
            pl.when(only)(cp.start)
        return cp

    loads = []
    for b in range(SBLK):
        loads.append((
            pltpu.make_async_copy(anterp.at[:, b], an.at[:, b], ld.at[1, b]),
            pltpu.make_async_copy(charges.at[:, b], ch.at[:, b], ld.at[0, b])))
        if b < 2:
            for cp in loads[b]:
                cp.start()
    lv_loads = [
        pltpu.make_async_copy(levels.at[l, o], lv.at[l, :, :, :, pl.ds(o * R, R)], lvs.at[l, o])
        for l in range(2) for o in range(2)
    ]

    greet = [x_dev(d, e) for d, e in others] + level_dev + [z_dev, near_dev[1]]
    barrier = pltpu.get_barrier_semaphore()
    for dev in greet:
        pl.semaphore_signal(barrier, 1, device_id=dev, device_id_type=MESH)

    @pl.when(relay | relayed)
    def _():
        pl.semaphore_signal(barrier, 1, device_id=relay_dev, device_id_type=MESH)

    left, own, right = near[0, 0], near[0, 1], near[0, 2]
    nlv[0] = jnp.full((8, 128), jnp.where(c == 1, left, right), jnp.int32)
    nlv[1] = jnp.full((8, 128), jnp.where(c == 1, right, left), jnp.int32)

    def coefficients(b):
        for cp in loads[b]:
            cp.wait()
        for cp in loads[b + 2] if b + 2 < SBLK else lv_loads if b + 2 == SBLK else ():
            cp.start()
        re, im = cdot(an[0, b], an[1, b], ch[0, b], ch[1, b])
        v[0, b, 0, pl.ds(0, R), :] = re.astype(BF16)
        v[0, b, 1, pl.ds(0, R), :] = im.astype(BF16)

    coefficients(0)
    pl.semaphore_wait(barrier, len(greet) + (relay | relayed).astype(jnp.int32))
    nl_cp = [remote(nlv.at[i], nlr.at[i], nl_s.at[i], nl_r.at[i], near_dev[i]) for i in (1, 0)][::-1]

    w_cp = {}
    own_w = []
    for h in range(2):
        col = (x * 4 + h * 2 + c) * KB
        own_w.append(pltpu.make_async_copy(
            transfer.at[:, 0, :, pl.ds(pl.multiple_of(col, KB), KB)],
            w.at[:, pl.ds(0, R), pl.ds(h * KB, KB)], w_s.at[0, h]))

    def send_w(d, e):
        core = c if e == 0 else 1 - c
        slot = e * 4 + (-d) % 4
        for h in range(2):
            col = (((x + d) % 4) * 4 + h * 2 + core) * KB
            w_cp[slot, h] = remote(
                transfer.at[:, 0, :, pl.ds(pl.multiple_of(col, KB), KB)],
                w.at[:, pl.ds(slot * R, R), pl.ds(h * KB, KB)],
                w_s.at[slot, h], w_r.at[slot, h], x_dev(d, e))

    l_cp = {}

    def send_level(l, b):
        l_cp[l, b] = remote(
            v.at[l, b, :, pl.ds(0, R), :], v.at[l, b, :, pl.ds(R, R), :], l_s.at[l, b], l_r.at[l, b], level_dev[l])

    for b in range(SBLK):
        if b > 0:
            coefficients(b)
        send_level(0, b)

    for d, e in others:
        send_w(d, e)
    for cp in own_w:
        cp.start()

    nm = {}
    for i in (1, 0):
        nl_cp[i].wait_recv()
        nm[i] = pltpu.make_async_copy(nlr.at[i], nlm.at[i], nm_s.at[i])
        nm[i].start()
    xs_cp, n_cp, rl_cp = {}, {}, {}

    def pick(i):
        nm[i].wait()
        index = nlm[i, 0, 0]
        shift = BOX * (2 * c - 1).astype(F32)
        sxs[i, 0:1, :] = sxy[0, pl.ds(index, 1), :] + (shift if i == 0 else -shift)
        sxs[i, 1:2, :] = sxy[1, pl.ds(index, 1), :]

        def some(j, _):
            r = rows_at(j, 64)
            for q in range(2):
                ns[i, q, r, :] = ch[q, index, r, :]
            return 0

        lax.fori_loop(0, PTS // 64, some, 0)
        xs_cp[i] = remote(sxs.at[i], sxr.at[i], xs_s.at[i], xs_r.at[i], near_dev[i])

    def send_near(i, p, only=None):
        r = pl.ds(p * PIECE, PIECE)
        n_cp[i, p] = remote(
            ns.at[i, :, r, :], nr.at[i, :, r, :], n_s.at[i, p], n_r.at[i, p], near_dev[i], only)

    def send_crossing(p):
        if p < len(RELAYS):
            send_near(1, p, crossing & direct)
            r = pl.ds(p * PIECE, PIECE)
            rl_cp[p] = remote(ns.at[1, :, r, :], rl.at[p], n_s.at[1, p], rl_r.at[p], relay_dev, relayed)
        else:
            send_near(1, p, crossing & has_far)

    def pass_on(p):
        pl.when(relay)(rl_cp[p].wait_recv)
        r = pl.ds(p * PIECE, PIECE)
        remote(rl.at[p], nr.at[1, :, r, :], rl_s.at[p], n_r.at[1, p], relay_target, relay)

    def sends_at(place):
        for p in X_SENDS[place]:
            send_crossing(p)
        for p in Z_SENDS[place]:
            send_near(1, p, jnp.logical_not(crossing))
        for p, where in enumerate(RELAYS):
            if where == place:
                pass_on(p)

    pick(1)
    sends_at(0)
    pick(0)
    for p in range(NP):
        send_near(0, p)

    amp = 1.0 / (4.0 * math.pi)
    txt[...] = jnp.concatenate([txy[0], txy[1], jnp.zeros((6, PTS), F32)], 0).T
    sxs[2, 0:1, :] = sxy[0, pl.ds(own, 1), :]
    sxs[2, 1:2, :] = sxy[1, pl.ds(own, 1), :]

    def tiles(i, src, scale, first, count):
        def step(j, _):
            at_row = (first + j) * ROWS
            gen_tile(txt, src, scale, at_row, tc.at[i], ts.at[i], at_row)
            return 0
        lax.fori_loop(0, count, step, 0)

    def own_part(first, count):
        def row_step(j, _):
            r = rows_at(first + j, 256)
            acc[0, r, :], acc[1, r, :] = cdot(tc[0, r, :], ts[0, r, :], ch[0, own], ch[1, own])
            return 0
        lax.fori_loop(0, count, row_step, 0)

    def level_step(l, b):
        l_cp[l, b].wait_recv()
        re, im = cdot(lv[l, 0, b], lv[l, 1, b], v[l, b, 0], v[l, b, 1])
        if l == 0:
            v[1, b, 0, pl.ds(0, R), :] = re.astype(BF16)
            v[1, b, 1, pl.ds(0, R), :] = im.astype(BF16)
        else:
            r = pl.ds(pl.multiple_of(hi * KB + b * R, R), R)
            g[0, r, :] = re.astype(BF16)
            g[1, r, :] = im.astype(BF16)

    g_cp = {}
    for cp in lv_loads:
        cp.wait()
    for b in range(SBLK):
        tiles(0, sxs.at[2], amp, 2 * b, 2)
        level_step(0, b)
        send_level(1, b)
        sends_at(1 + b)
    for b in range(SBLK):
        own_part(b, 1)
        level_step(1, b)
        r = pl.ds(pl.multiple_of(hi * KB + b * R, R), R)
        g_cp[b] = remote(g.at[:, r, :], g.at[:, r, :], g_s.at[b], g_r.at[b], z_dev)
        sends_at(5 + b)

    far_amp = jnp.where((t == 0) | (t == 15), 0.0, amp)

    def far_part(p):
        cols = pl.ds(p * PIECE, PIECE)

        def row_step(j, _):
            r = rows_at(j, 512)
            re, im = cdot(tc[1, r, cols], ts[1, r, cols], nr[1, 0, cols, :], nr[1, 1, cols, :])
            acc[0, r, :] += re
            acc[1, r, :] += im
            return 0

        n_cp[1, p].wait_recv()
        lax.fori_loop(0, PTS // 512, row_step, 0)

    xs_cp[0].wait_recv()
    tiles(0, sxr.at[0], amp, 0, 8)
    for p in range(NP):
        n_cp[0, p].wait_recv()

    def sib_step(j, _):
        r = rows_at(j, 256)
        re, im = cdot(tc[0, r, :], ts[0, r, :], nr[0, 0], nr[0, 1])
        acc[0, r, :] += re
        acc[1, r, :] += im
        return 0

    lax.fori_loop(0, PTS // 256, sib_step, 0)
    xs_cp[1].wait_recv()
    tiles(1, sxr.at[1], far_amp, 0, 8)
    last = pl.ds((NP - 1) * PIECE, PIECE)
    outs = [
        pltpu.make_async_copy(tc.at[1, :, last], tile_out.at[0], o_s.at[0]),
        pltpu.make_async_copy(ts.at[1, :, last], tile_out.at[1], o_s.at[1]),
    ]
    for cp in outs:
        cp.start()

    q_cp, p_cp = {}, {}
    for cp in own_w:
        cp.wait()
    for cp in w_cp.values():
        cp.wait_recv()
    for b in range(SBLK):
        g_cp[b].wait_recv()
    sends_at(9)

    def partial(e, k):
        cols = pl.ds(k * CW, CW)
        r = pl.ds(e * 4 * R, 4 * R)
        return cdot(w[0, r, :], w[1, r, :], g[0, :, cols], g[1, :, cols])

    def for_sibling(k):
        for q, part in enumerate(partial(1, k)):
            qs[k, :, q] = part.astype(BF16).reshape(4, R, CW)
        q_cp[k] = remote(qs.at[k], qr.at[k], q_s.at[k], q_r.at[k], near_dev[0])

    def for_targets(k):
        for q, part in enumerate(partial(0, k)):
            pf[q] = part.reshape(4, R, CW)
        q_cp[k].wait_recv()
        for q in range(2):
            ps[k, :, q] = (pf[q] + qr[k, :, q].astype(F32)).astype(BF16)
        for d in (1, 3, 2):
            p_cp[k, d] = remote(
                ps.at[k, d], pr.at[k, 4 - d], p_s.at[k, d], p_r.at[k, 4 - d], x_dev(d, 0))

    for k in range(NC):
        for_sibling(k)
    for k in range(NC):
        for_targets(k)

    def middle(k):
        cols = pl.ds(k * CW, CW)
        for d in (1, 2, 3):
            p_cp[k, d].wait_recv()
        for q in range(2):
            total = ps[k, 0, q].astype(F32)
            for d in (1, 2, 3):
                total = total + pr[k, d, q].astype(F32)
            if q == 0:
                mid[0, pl.ds(0, R), cols] = total.astype(BF16)
                mid[1, pl.ds(R, R), cols] = total.astype(BF16)
            else:
                mid[0, pl.ds(R, R), cols] = (-total).astype(BF16)
                mid[1, pl.ds(0, R), cols] = total.astype(BF16)

    for p in range(NP - 1):
        pl.when(has_far)(functools.partial(far_part, p))
    rounded[...] = acc[...].astype(BF16)
    outs.append(pltpu.make_async_copy(rounded, near_out, o_s.at[2]))
    outs[2].start()
    for k in range(NC):
        middle(k)

    @pl.when(relay)
    def _():
        nr[1, :, last, :] = jnp.zeros((2, PIECE, NR), BF16)

    pl.when(has_far)(n_cp[1, NP - 1].wait_recv)
    outs.append(pltpu.make_async_copy(nr.at[1, :, last, :], piece_out, o_s.at[3]))
    outs[3].start()
    for cp in outs:
        cp.wait()
    for only, cp in pending:
        if only is None:
            cp.wait_send()
        else:
            pl.when(only)(cp.wait_send)


def finish_kernel(near, tile, piece, mid, evaluate, out, nv, tv, pv, mv, ev, ov, n_l, t_l, p_l, m_l, e_l, o_s):
    dot = functools.partial(jnp.dot, preferred_element_type=F32)
    steps = n_l.shape[0]
    rows = PTS // steps
    whole = [pltpu.make_async_copy(piece, pv, p_l), pltpu.make_async_copy(mid, mv, m_l)]
    loads = []
    for j in range(steps):
        r = pl.ds(j * rows, rows)
        loads.append([
            pltpu.make_async_copy(tile.at[:, r, :], tv.at[:, r, :], t_l.at[j]),
            pltpu.make_async_copy(evaluate.at[:, 0, r, :], ev.at[:, r, :], e_l.at[j]),
            pltpu.make_async_copy(near.at[:, r, :], nv.at[:, r, :], n_l.at[j]),
        ])
    for cp in whole + [cp for load in loads for cp in load]:
        cp.start()
    for cp in whole:
        cp.wait()
    stores = []
    for j in range(steps):
        for cp in loads[j]:
            cp.wait()
        r = pl.ds(j * rows, rows)
        er_ei = jnp.concatenate([ev[0, r, :], ev[1, r, :]], 1)
        for q in range(2):
            if q == 0:
                part = dot(tv[0, r, :], pv[0]) - dot(tv[1, r, :], pv[1])
            else:
                part = dot(tv[0, r, :], pv[1]) + dot(tv[1, r, :], pv[0])
            ov[q, r, :] = nv[q, r, :].astype(F32) + part + dot(er_ei, mv[q])
            stores.append(pltpu.make_async_copy(ov.at[q, r, :], out.at[q, 0, r, :], o_s.at[j, q]))
            stores[-1].start()
    for cp in stores:
        cp.wait()


RELAYS = (7, 8)
X_SENDS = ((), (0,), (1,), (2,), (), (3,), (), (), (), ())
Z_SENDS = ((), (), (), (), (), (), (), (), (0,), (1, 2, 3))


def shards(charges, source_xy, target_xy, anterp, levels, transfer, evaluate, near_list):
    vmem = pl.BlockSpec(memory_space=pltpu.VMEM)
    hbm = pl.BlockSpec(memory_space=pl.ANY)
    dma = pltpu.SemaphoreType.DMA
    near, tile, piece, mid = pl.pallas_call(
        main_kernel,
        out_shape=(
            jax.ShapeDtypeStruct((2, PTS, NR), BF16),
            jax.ShapeDtypeStruct((2, PTS, PIECE), BF16),
            jax.ShapeDtypeStruct((2, PIECE, NR), BF16),
            jax.ShapeDtypeStruct((2, 2 * R, NR), BF16),
        ),
        in_specs=[pl.BlockSpec(memory_space=pltpu.SMEM), vmem, vmem, hbm, hbm, hbm, hbm],
        out_specs=(hbm, hbm, hbm, vmem),
        scratch_shapes=[
            pltpu.VMEM((2, SBLK, PTS, NR), BF16),
            pltpu.VMEM((2, SBLK, R, PTS), BF16),
            pltpu.VMEM((2, 2, SBLK, R, 2 * R), BF16),
            pltpu.VMEM((2, 8 * R, 2 * KB), BF16),
            pltpu.VMEM((2, SBLK, 2, 2 * R, NR), BF16),
            pltpu.VMEM((2, 2 * KB, NR), BF16),
            pltpu.VMEM((NC, 4, 2, R, CW), BF16),
            pltpu.VMEM((NC, 4, 2, R, CW), BF16),
            pltpu.VMEM((2, 4, R, CW), F32),
            pltpu.VMEM((NC, 4, 2, R, CW), BF16),
            pltpu.VMEM((NC, 4, 2, R, CW), BF16),
            pltpu.VMEM((2, 2, PTS, NR), BF16),
            pltpu.VMEM((2, 2, PTS, NR), BF16),
            pltpu.VMEM((2, 2, PIECE, NR), BF16),
            pltpu.VMEM((2, 8, 128), jnp.int32),
            pltpu.VMEM((2, 8, 128), jnp.int32),
            pltpu.SMEM((2, 8, 128), jnp.int32),
            pltpu.VMEM((3, 2, PTS), F32),
            pltpu.VMEM((2, 2, PTS), F32),
            pltpu.VMEM((PTS, 8), F32),
            pltpu.VMEM((2, PTS, PTS), BF16),
            pltpu.VMEM((2, PTS, PTS), BF16),
            pltpu.VMEM((2, PTS, NR), F32),
            pltpu.VMEM((2, PTS, NR), BF16),
            dma((2, SBLK)), dma((2, 2)), dma((2,)), dma((2,)), dma((2,)), dma((2,)), dma((2,)),
            dma((8, 2)), dma((8, 2)), dma((2, SBLK)), dma((2, SBLK)), dma((SBLK,)), dma((SBLK,)),
            dma((NC,)), dma((NC,)), dma((NC, 4)), dma((NC, 4)), dma((2, NP)), dma((2, NP)), dma((2,)), dma((2,)), dma((4,)),
        ],
        compiler_params=pltpu.CompilerParams(
            collective_id=0, has_side_effects=True, vmem_limit_bytes=60 * 2**20),
        name="field_kernel",
    )(near_list, source_xy, target_xy, charges, anterp, levels, transfer)
    steps = 2
    return pl.pallas_call(
        finish_kernel,
        out_shape=jax.ShapeDtypeStruct((2, 1, PTS, NR), F32),
        in_specs=[hbm] * 5,
        out_specs=hbm,
        scratch_shapes=[
            pltpu.VMEM((2, PTS, NR), BF16),
            pltpu.VMEM((2, PTS, PIECE), BF16),
            pltpu.VMEM((2, PIECE, NR), BF16),
            pltpu.VMEM((2, 2 * R, NR), BF16),
            pltpu.VMEM((2, PTS, R), BF16),
            pltpu.VMEM((2, PTS, NR), F32),
            dma((steps,)), dma((steps,)), dma, dma, dma((steps,)), dma((steps, 2)),
        ],
        compiler_params=pltpu.CompilerParams(vmem_limit_bytes=60 * 2**20),
        name="finish_kernel",
    )(near, tile, piece, mid, evaluate)


def solution(mesh):
    return jax.shard_map(
        shards,
        mesh=mesh,
        in_specs=(
            P(None, ("src", "tgt"), None, None),
            P(None, ("src", "tgt"), None),
            P(None, ("src", "tgt"), None),
            P(None, ("src", "tgt"), None, None),
            P(None, None, None, ("src", "tgt"), None, None),
            P(None, ("src", "tgt"), None, None),
            P(None, ("src", "tgt"), None, None),
            P(("src", "tgt"), None),
        ),
        out_specs=P(None, ("src", "tgt"), None, None),
        check_vma=False,
    )
```

```python
import functools
import math

import jax
import jax.numpy as jnp
from jax import lax
from jax.experimental import pallas as pl
from jax.experimental.pallas import tpu as pltpu
from jax.sharding import PartitionSpec as P

KAPPA = 73.27
CORE = 0.5
BOX = 8.0
MESH = pl.DeviceIdType.MESH
F32, BF16 = jnp.float32, jnp.bfloat16

PTS, R, NR, SBLK = 1024, 128, 512, 4
KB = SBLK * R
NC = 2
CW = NR // NC
ROWS = 128
PIECE = 256
NP = PTS // PIECE
COS = (0.99999922, -19.73898252, 64.92872657, -85.2723964, 58.79403555, -21.07677646)
SIN = (6.2830558, -41.33121426, 81.36681443, -74.47799927, 32.78139018)


def horner(coefs, u):
    out = coefs[-1]
    for c in coefs[-2::-1]:
        out = out * u + c
    return out


def cdot(ar, ai, xr, xi):
    dot = functools.partial(jnp.dot, preferred_element_type=F32)
    return dot(ar, xr) - dot(ai, xi), dot(ar, xi) + dot(ai, xr)


def rows_at(i, n):
    if isinstance(i, int):
        return pl.ds(i * n, n)
    return pl.ds(pl.multiple_of(i * n, n), n)


def gen_tile(txy, src, scale, row0, cos_ref, sin_ref, at):
    wide = 256

    def group(i, _):
        r = pl.ds(pl.multiple_of(row0 + i * 16, 16), 16)
        o = pl.ds(pl.multiple_of(at + i * 16, 16), 16)
        tx, ty = txy[r, 0:1], txy[r, 1:2]
        for j in range(PTS // wide):
            c = slice(j * wide, (j + 1) * wide)
            dx = tx - src[0:1, c]
            dy = ty - src[1:2, c]
            r2 = dx * dx + (dy * dy + CORE * CORE)
            inv = lax.rsqrt(r2)
            inv = inv * (1.5 - (0.5 * r2) * (inv * inv))
            turns = (r2 * inv) * (KAPPA / (2.0 * math.pi))
            f = turns - jnp.round(turns)
            u = f * f
            amp = inv * scale
            cos_ref[o, c] = (horner(COS, u) * amp).astype(BF16)
            sin_ref[o, c] = (horner(SIN, u) * (f * amp)).astype(BF16)
        return 0

    lax.fori_loop(0, ROWS // 16, group, 0)


def main_kernel(
    near, sxy, txy, charges, anterp, levels, transfer, near_out, tile_out, piece_out, mid,
    ch, an, lv, w, v, g, qs, qr, pf, ps, pr, ns, nr, rl, nlv, nlr, nlm, sxs, sxr, txt, tc, ts, acc, rounded,
    ld, lvs, nl_s, nl_r, nm_s, xs_s, xs_r, w_s, w_r, l_s, l_r, g_s, g_r, q_s, q_r, p_s, p_r, n_s, n_r, rl_s, rl_r, o_s,
):
    s, t = lax.axis_index("src"), lax.axis_index("tgt")
    n_src = 8
    c = t % 2
    hi = (t // 2) % 2
    x = t // 4

    def at(src, tgt):
        return {"src": src, "tgt": tgt}

    near_dev = [at(s, t + 1 - 2 * c), at(s, (t + 15 + 2 * c) % 16)]
    level_dev = [at((s + n_src // 2) % n_src, t), at(s // 4 * 4 + (s + 2) % 4, t)]
    z_dev = at(s, x * 4 + (1 - hi) * 2 + c)

    has_far = (t != 0) & (t != 15)
    relay = jnp.logical_not(has_far)
    relayed = (t == 3) | (t == 12)
    crossing = hi == c
    direct = has_far & jnp.logical_not(relayed)
    relay_dev = at(s, jnp.where(x == 0, 3 - t, jnp.where(x == 3, 27 - t, t)))
    relay_target = at(s, jnp.where(x == 0, 4, 11))

    def x_dev(d, e):
        core = c if e == 0 else 1 - c
        return at(s, ((x + d) % 4) * 4 + hi * 2 + core)

    others = [(d, e) for d in (1, 3, 2, 0) for e in (0, 1) if (d, e) != (0, 0)]
    pending = []

    def remote(src, dst, ss, rs, dev, only=None):
        cp = pltpu.make_async_remote_copy(src, dst, ss, rs, device_id=dev, device_id_type=MESH)
        pending.append((only, cp))
        if only is None:
            cp.start()
        else:
            pl.when(only)(cp.start)
        return cp

    loads = []
    for b in range(SBLK):
        loads.append((
            pltpu.make_async_copy(anterp.at[:, b], an.at[:, b], ld.at[1, b]),
            pltpu.make_async_copy(charges.at[:, b], ch.at[:, b], ld.at[0, b])))
        if b < 2:
            for cp in loads[b]:
                cp.start()
    lv_loads = [
        pltpu.make_async_copy(levels.at[l, o], lv.at[l, :, :, :, pl.ds(o * R, R)], lvs.at[l, o])
        for l in range(2) for o in range(2)
    ]

    greet = [x_dev(d, e) for d, e in others] + level_dev + [z_dev, near_dev[1]]
    barrier = pltpu.get_barrier_semaphore()
    for dev in greet:
        pl.semaphore_signal(barrier, 1, device_id=dev, device_id_type=MESH)

    @pl.when(relay | relayed)
    def _():
        pl.semaphore_signal(barrier, 1, device_id=relay_dev, device_id_type=MESH)

    left, own, right = near[0, 0], near[0, 1], near[0, 2]
    nlv[0] = jnp.full((8, 128), jnp.where(c == 1, left, right), jnp.int32)
    nlv[1] = jnp.full((8, 128), jnp.where(c == 1, right, left), jnp.int32)

    def coefficients(b):
        for cp in loads[b]:
            cp.wait()
        for cp in loads[b + 2] if b + 2 < SBLK else lv_loads if b + 2 == SBLK else ():
            cp.start()
        re, im = cdot(an[0, b], an[1, b], ch[0, b], ch[1, b])
        v[0, b, 0, pl.ds(0, R), :] = re.astype(BF16)
        v[0, b, 1, pl.ds(0, R), :] = im.astype(BF16)

    coefficients(0)
    pl.semaphore_wait(barrier, len(greet) + (relay | relayed).astype(jnp.int32))
    nl_cp = [remote(nlv.at[i], nlr.at[i], nl_s.at[i], nl_r.at[i], near_dev[i]) for i in (1, 0)][::-1]

    w_cp = {}
    own_w = []
    for h in range(2):
        col = (x * 4 + h * 2 + c) * KB
        own_w.append(pltpu.make_async_copy(
            transfer.at[:, 0, :, pl.ds(pl.multiple_of(col, KB), KB)],
            w.at[:, pl.ds(0, R), pl.ds(h * KB, KB)], w_s.at[0, h]))

    def send_w(d, e):
        core = c if e == 0 else 1 - c
        slot = e * 4 + (-d) % 4
        for h in range(2):
            col = (((x + d) % 4) * 4 + h * 2 + core) * KB
            w_cp[slot, h] = remote(
                transfer.at[:, 0, :, pl.ds(pl.multiple_of(col, KB), KB)],
                w.at[:, pl.ds(slot * R, R), pl.ds(h * KB, KB)],
                w_s.at[slot, h], w_r.at[slot, h], x_dev(d, e))

    l_cp = {}

    def send_level(l, b):
        l_cp[l, b] = remote(
            v.at[l, b, :, pl.ds(0, R), :], v.at[l, b, :, pl.ds(R, R), :], l_s.at[l, b], l_r.at[l, b], level_dev[l])

    for b in range(SBLK):
        if b > 0:
            coefficients(b)
        send_level(0, b)

    for d, e in others:
        send_w(d, e)
    for cp in own_w:
        cp.start()

    nm = {}
    for i in (1, 0):
        nl_cp[i].wait_recv()
        nm[i] = pltpu.make_async_copy(nlr.at[i], nlm.at[i], nm_s.at[i])
        nm[i].start()
    xs_cp, n_cp, rl_cp = {}, {}, {}

    def pick(i):
        nm[i].wait()
        index = nlm[i, 0, 0]
        shift = BOX * (2 * c - 1).astype(F32)
        sxs[i, 0:1, :] = sxy[0, pl.ds(index, 1), :] + (shift if i == 0 else -shift)
        sxs[i, 1:2, :] = sxy[1, pl.ds(index, 1), :]

        def some(j, _):
            r = rows_at(j, 64)
            for q in range(2):
                ns[i, q, r, :] = ch[q, index, r, :]
            return 0

        lax.fori_loop(0, PTS // 64, some, 0)
        xs_cp[i] = remote(sxs.at[i], sxr.at[i], xs_s.at[i], xs_r.at[i], near_dev[i])

    def send_near(i, p, only=None):
        r = pl.ds(p * PIECE, PIECE)
        n_cp[i, p] = remote(
            ns.at[i, :, r, :], nr.at[i, :, r, :], n_s.at[i, p], n_r.at[i, p], near_dev[i], only)

    def send_crossing(p):
        if p < len(RELAYS):
            send_near(1, p, crossing & direct)
            r = pl.ds(p * PIECE, PIECE)
            rl_cp[p] = remote(ns.at[1, :, r, :], rl.at[p], n_s.at[1, p], rl_r.at[p], relay_dev, relayed)
        else:
            send_near(1, p, crossing & has_far)

    def pass_on(p):
        pl.when(relay)(rl_cp[p].wait_recv)
        r = pl.ds(p * PIECE, PIECE)
        remote(rl.at[p], nr.at[1, :, r, :], rl_s.at[p], n_r.at[1, p], relay_target, relay)

    def sends_at(place):
        for p in X_SENDS[place]:
            send_crossing(p)
        for p in Z_SENDS[place]:
            send_near(1, p, jnp.logical_not(crossing))
        for p, where in enumerate(RELAYS):
            if where == place:
                pass_on(p)

    pick(1)
    sends_at(0)
    pick(0)
    for p in range(NP):
        send_near(0, p)

    amp = 1.0 / (4.0 * math.pi)
    txt[...] = jnp.concatenate([txy[0], txy[1], jnp.zeros((6, PTS), F32)], 0).T
    sxs[2, 0:1, :] = sxy[0, pl.ds(own, 1), :]
    sxs[2, 1:2, :] = sxy[1, pl.ds(own, 1), :]

    def tiles(i, src, scale, first, count):
        def step(j, _):
            at_row = (first + j) * ROWS
            gen_tile(txt, src, scale, at_row, tc.at[i], ts.at[i], at_row)
            return 0
        lax.fori_loop(0, count, step, 0)

    def own_part(first, count):
        def row_step(j, _):
            r = rows_at(first + j, 256)
            acc[0, r, :], acc[1, r, :] = cdot(tc[0, r, :], ts[0, r, :], ch[0, own], ch[1, own])
            return 0
        lax.fori_loop(0, count, row_step, 0)

    def level_step(l, b):
        l_cp[l, b].wait_recv()
        re, im = cdot(lv[l, 0, b], lv[l, 1, b], v[l, b, 0], v[l, b, 1])
        if l == 0:
            v[1, b, 0, pl.ds(0, R), :] = re.astype(BF16)
            v[1, b, 1, pl.ds(0, R), :] = im.astype(BF16)
        else:
            r = pl.ds(pl.multiple_of(hi * KB + b * R, R), R)
            g[0, r, :] = re.astype(BF16)
            g[1, r, :] = im.astype(BF16)

    g_cp = {}
    for cp in lv_loads:
        cp.wait()
    for b in range(SBLK):
        tiles(0, sxs.at[2], amp, 2 * b, 2)
        level_step(0, b)
        send_level(1, b)
        sends_at(1 + b)
    for b in range(SBLK):
        own_part(b, 1)
        level_step(1, b)
        r = pl.ds(pl.multiple_of(hi * KB + b * R, R), R)
        g_cp[b] = remote(g.at[:, r, :], g.at[:, r, :], g_s.at[b], g_r.at[b], z_dev)
        sends_at(5 + b)

    far_amp = jnp.where((t == 0) | (t == 15), 0.0, amp)

    def far_part(p):
        cols = pl.ds(p * PIECE, PIECE)

        def row_step(j, _):
            r = rows_at(j, 512)
            re, im = cdot(tc[1, r, cols], ts[1, r, cols], nr[1, 0, cols, :], nr[1, 1, cols, :])
            acc[0, r, :] += re
            acc[1, r, :] += im
            return 0

        n_cp[1, p].wait_recv()
        lax.fori_loop(0, PTS // 512, row_step, 0)

    xs_cp[0].wait_recv()
    tiles(0, sxr.at[0], amp, 0, 8)
    sends_at(10)
    for p in range(NP):
        n_cp[0, p].wait_recv()

    def sib_step(j, _):
        r = rows_at(j, 256)
        re, im = cdot(tc[0, r, :], ts[0, r, :], nr[0, 0], nr[0, 1])
        acc[0, r, :] += re
        acc[1, r, :] += im
        return 0

    lax.fori_loop(0, PTS // 256, sib_step, 0)
    sends_at(11)
    xs_cp[1].wait_recv()
    tiles(1, sxr.at[1], far_amp, 0, 8)
    last = pl.ds((NP - 1) * PIECE, PIECE)
    outs = [
        pltpu.make_async_copy(tc.at[1, :, last], tile_out.at[0], o_s.at[0]),
        pltpu.make_async_copy(ts.at[1, :, last], tile_out.at[1], o_s.at[1]),
    ]
    for cp in outs:
        cp.start()

    q_cp, p_cp = {}, {}
    for cp in own_w:
        cp.wait()
    for cp in w_cp.values():
        cp.wait_recv()
    for b in range(SBLK):
        g_cp[b].wait_recv()
    sends_at(9)

    def partial(e, k):
        cols = pl.ds(k * CW, CW)
        r = pl.ds(e * 4 * R, 4 * R)
        return cdot(w[0, r, :], w[1, r, :], g[0, :, cols], g[1, :, cols])

    def for_sibling(k):
        for q, part in enumerate(partial(1, k)):
            qs[k, :, q] = part.astype(BF16).reshape(4, R, CW)
        q_cp[k] = remote(qs.at[k], qr.at[k], q_s.at[k], q_r.at[k], near_dev[0])

    def for_targets(k):
        for q, part in enumerate(partial(0, k)):
            pf[q] = part.reshape(4, R, CW)
        q_cp[k].wait_recv()
        for q in range(2):
            ps[k, :, q] = (pf[q] + qr[k, :, q].astype(F32)).astype(BF16)
        for d in (1, 3, 2):
            p_cp[k, d] = remote(
                ps.at[k, d], pr.at[k, 4 - d], p_s.at[k, d], p_r.at[k, 4 - d], x_dev(d, 0))

    for k in range(NC):
        for_sibling(k)
    for k in range(NC):
        for_targets(k)

    def middle(k):
        cols = pl.ds(k * CW, CW)
        for d in (1, 2, 3):
            p_cp[k, d].wait_recv()
        for q in range(2):
            total = ps[k, 0, q].astype(F32)
            for d in (1, 2, 3):
                total = total + pr[k, d, q].astype(F32)
            if q == 0:
                mid[0, pl.ds(0, R), cols] = total.astype(BF16)
                mid[1, pl.ds(R, R), cols] = total.astype(BF16)
            else:
                mid[0, pl.ds(R, R), cols] = (-total).astype(BF16)
                mid[1, pl.ds(0, R), cols] = total.astype(BF16)

    for p in range(NP - 1):
        pl.when(has_far)(functools.partial(far_part, p))
    rounded[...] = acc[...].astype(BF16)
    outs.append(pltpu.make_async_copy(rounded, near_out, o_s.at[2]))
    outs[2].start()
    for k in range(NC):
        middle(k)

    @pl.when(relay)
    def _():
        nr[1, :, last, :] = jnp.zeros((2, PIECE, NR), BF16)

    pl.when(has_far)(n_cp[1, NP - 1].wait_recv)
    outs.append(pltpu.make_async_copy(nr.at[1, :, last, :], piece_out, o_s.at[3]))
    outs[3].start()
    for cp in outs:
        cp.wait()
    for only, cp in pending:
        if only is None:
            cp.wait_send()
        else:
            pl.when(only)(cp.wait_send)


def finish_kernel(near, tile, piece, mid, evaluate, out, nv, tv, pv, mv, ev, ov, n_l, t_l, p_l, m_l, e_l, o_s):
    dot = functools.partial(jnp.dot, preferred_element_type=F32)
    steps = n_l.shape[0]
    rows = PTS // steps
    whole = [pltpu.make_async_copy(piece, pv, p_l), pltpu.make_async_copy(mid, mv, m_l)]
    loads = []
    for j in range(steps):
        r = pl.ds(j * rows, rows)
        loads.append([
            pltpu.make_async_copy(tile.at[:, r, :], tv.at[:, r, :], t_l.at[j]),
            pltpu.make_async_copy(evaluate.at[:, 0, r, :], ev.at[:, r, :], e_l.at[j]),
            pltpu.make_async_copy(near.at[:, r, :], nv.at[:, r, :], n_l.at[j]),
        ])
    for cp in whole + [cp for load in loads for cp in load]:
        cp.start()
    for cp in whole:
        cp.wait()
    stores = []
    for j in range(steps):
        for cp in loads[j]:
            cp.wait()
        r = pl.ds(j * rows, rows)
        er_ei = jnp.concatenate([ev[0, r, :], ev[1, r, :]], 1)
        for q in range(2):
            if q == 0:
                part = dot(tv[0, r, :], pv[0]) - dot(tv[1, r, :], pv[1])
            else:
                part = dot(tv[0, r, :], pv[1]) + dot(tv[1, r, :], pv[0])
            ov[q, r, :] = nv[q, r, :].astype(F32) + part + dot(er_ei, mv[q])
            stores.append(pltpu.make_async_copy(ov.at[q, r, :], out.at[q, 0, r, :], o_s.at[j, q]))
            stores[-1].start()
    for cp in stores:
        cp.wait()


RELAYS = (7, 8)
X_SENDS = ((), (0,), (1,), (2,), (), (3,), (), (), (), (), (), ())
Z_SENDS = ((), (), (), (), (), (), (), (), (0,), (3,), (1,), (2,))


def shards(charges, source_xy, target_xy, anterp, levels, transfer, evaluate, near_list):
    vmem = pl.BlockSpec(memory_space=pltpu.VMEM)
    hbm = pl.BlockSpec(memory_space=pl.ANY)
    dma = pltpu.SemaphoreType.DMA
    near, tile, piece, mid = pl.pallas_call(
        main_kernel,
        out_shape=(
            jax.ShapeDtypeStruct((2, PTS, NR), BF16),
            jax.ShapeDtypeStruct((2, PTS, PIECE), BF16),
            jax.ShapeDtypeStruct((2, PIECE, NR), BF16),
            jax.ShapeDtypeStruct((2, 2 * R, NR), BF16),
        ),
        in_specs=[pl.BlockSpec(memory_space=pltpu.SMEM), vmem, vmem, hbm, hbm, hbm, hbm],
        out_specs=(hbm, hbm, hbm, vmem),
        scratch_shapes=[
            pltpu.VMEM((2, SBLK, PTS, NR), BF16),
            pltpu.VMEM((2, SBLK, R, PTS), BF16),
            pltpu.VMEM((2, 2, SBLK, R, 2 * R), BF16),
            pltpu.VMEM((2, 8 * R, 2 * KB), BF16),
            pltpu.VMEM((2, SBLK, 2, 2 * R, NR), BF16),
            pltpu.VMEM((2, 2 * KB, NR), BF16),
            pltpu.VMEM((NC, 4, 2, R, CW), BF16),
            pltpu.VMEM((NC, 4, 2, R, CW), BF16),
            pltpu.VMEM((2, 4, R, CW), F32),
            pltpu.VMEM((NC, 4, 2, R, CW), BF16),
            pltpu.VMEM((NC, 4, 2, R, CW), BF16),
            pltpu.VMEM((2, 2, PTS, NR), BF16),
            pltpu.VMEM((2, 2, PTS, NR), BF16),
            pltpu.VMEM((2, 2, PIECE, NR), BF16),
            pltpu.VMEM((2, 8, 128), jnp.int32),
            pltpu.VMEM((2, 8, 128), jnp.int32),
            pltpu.SMEM((2, 8, 128), jnp.int32),
            pltpu.VMEM((3, 2, PTS), F32),
            pltpu.VMEM((2, 2, PTS), F32),
            pltpu.VMEM((PTS, 8), F32),
            pltpu.VMEM((2, PTS, PTS), BF16),
            pltpu.VMEM((2, PTS, PTS), BF16),
            pltpu.VMEM((2, PTS, NR), F32),
            pltpu.VMEM((2, PTS, NR), BF16),
            dma((2, SBLK)), dma((2, 2)), dma((2,)), dma((2,)), dma((2,)), dma((2,)), dma((2,)),
            dma((8, 2)), dma((8, 2)), dma((2, SBLK)), dma((2, SBLK)), dma((SBLK,)), dma((SBLK,)),
            dma((NC,)), dma((NC,)), dma((NC, 4)), dma((NC, 4)), dma((2, NP)), dma((2, NP)), dma((2,)), dma((2,)), dma((4,)),
        ],
        compiler_params=pltpu.CompilerParams(
            collective_id=0, has_side_effects=True, vmem_limit_bytes=60 * 2**20),
        name="field_kernel",
    )(near_list, source_xy, target_xy, charges, anterp, levels, transfer)
    steps = 2
    return pl.pallas_call(
        finish_kernel,
        out_shape=jax.ShapeDtypeStruct((2, 1, PTS, NR), F32),
        in_specs=[hbm] * 5,
        out_specs=hbm,
        scratch_shapes=[
            pltpu.VMEM((2, PTS, NR), BF16),
            pltpu.VMEM((2, PTS, PIECE), BF16),
            pltpu.VMEM((2, PIECE, NR), BF16),
            pltpu.VMEM((2, 2 * R, NR), BF16),
            pltpu.VMEM((2, PTS, R), BF16),
            pltpu.VMEM((2, PTS, NR), F32),
            dma((steps,)), dma((steps,)), dma, dma, dma((steps,)), dma((steps, 2)),
        ],
        compiler_params=pltpu.CompilerParams(vmem_limit_bytes=60 * 2**20),
        name="finish_kernel",
    )(near, tile, piece, mid, evaluate)


def solution(mesh):
    return jax.shard_map(
        shards,
        mesh=mesh,
        in_specs=(
            P(None, ("src", "tgt"), None, None),
            P(None, ("src", "tgt"), None),
            P(None, ("src", "tgt"), None),
            P(None, ("src", "tgt"), None, None),
            P(None, None, None, ("src", "tgt"), None, None),
            P(None, ("src", "tgt"), None, None),
            P(None, ("src", "tgt"), None, None),
            P(("src", "tgt"), None),
        ),
        out_specs=P(None, ("src", "tgt"), None, None),
        check_vma=False,
    )
```
